32 devices in a mesh: groups: 2 (over y), wide: 8 (over z, x), narrow: 2 (over core).
Axes of the slice: x: 2, y: 2, z: 4, core: 2. Of those that a mesh axis runs over, the one named last changes fastest.
Arguments:
- traces: bfloat16 [256, 4096, 256], P(None, ('groups', 'wide'), 'narrow'), parts along dimension 1, may hold values from -6 to 6
- row_counts: int32 [16, 16], P(('groups', 'wide')), parts along dimension 0, may hold values from 1 to 8, as said below
- tile_cols: int32 [16, 80], P(('groups', 'wide')), parts along dimension 0, may hold values from 0 to 15, as said below
- tiles: bfloat16 [16, 80, 2, 128, 128], P(('groups', 'wide'), 'narrow'), parts along dimension 0, may hold values from -0.15625 to 0.15625
Outputs:
- redatumed_traces: bfloat16 [256, 4096, 256], P(None, ('groups', 'wide'), 'narrow'), parts along dimension 1
The draws below stay inside these ranges and needn't reach their ends.
There are 2 independent parts, one for each index of `groups`. The reference program is written for one: setup_inputs(seed, part) draws one part's arguments, and reference() takes and returns one part's arrays. A program takes and returns all parts, laid end to end along the dimension named above; each array names one. Nothing has to cross between parts.
Inputs may be any that keep to these rules, and one draw needn't show every extreme that they name: `row_counts`: for each frequency the 16 counts sum to at most 80, and to exactly 80 for at least one frequency; every frequency has a row with 8. A frequency's kept tiles fill its first slots, the rows one after another in order. `tile_cols`: the live slots of one tile row name different tile columns; slots past a frequency's total are not read.
All inputs are finite; a program needn't handle non-finite values.
Results may differ from the reference program's by a relative error of at most 0.012.
Values may be sent and summed in bfloat16 or wider, within the bound.
No kernel may reach another device: no remote copies, remote signals or barrier semaphores. Data moves between devices by JAX's collectives and lax.ppermute only.
A program may use at most 128 MiB of HBM per device.

```python
import math
import jax
import jax.numpy as jnp
from jax import lax

NT = 256
TILE = 128
R = 2048
V = 256
MAXROW = 8
KCAP = 80
F = 8
TBLK = 16
KHALF = 40


def tile_layout(key):
    key_list = jax.random.split(jax.random.fold_in(key, 11), 5)
    lowest = max(TBLK + MAXROW - 1, 3 * KCAP // 5)
    totals = jax.random.randint(key_list[0], (F,), lowest, KCAP + 1, dtype=jnp.int32)
    fullest = jax.random.randint(key_list[1], (), 0, F, dtype=jnp.int32)
    totals = jnp.where(jnp.arange(F, dtype=jnp.int32) == fullest, KCAP, totals).astype(jnp.int32)
    forced = jax.random.randint(key_list[2], (F,), 0, TBLK, dtype=jnp.int32)
    extra = MAXROW - 1
    unit_count = TBLK * extra
    unit_ids = jnp.arange(unit_count, dtype=jnp.int32)
    unit_rows = unit_ids // extra
    scores = jax.random.randint(key_list[3], (F, unit_count), 0, 1 << 20, dtype=jnp.int32) * unit_count + unit_ids[None, :] + unit_count
    scores = jnp.where(unit_rows[None, :] == forced[:, None], unit_ids[None, :], scores)
    unit_ranks = jnp.argsort(jnp.argsort(scores, axis=1), axis=1).astype(jnp.int32)
    chosen = (unit_ranks < (totals - TBLK)[:, None]).astype(jnp.int32)
    counts = (1 + jnp.sum(chosen.reshape(F, TBLK, extra), axis=2)).astype(jnp.int32)
    col_scores = jax.random.randint(key_list[4], (F, TBLK, TBLK), 0, 1 << 20, dtype=jnp.int32) * TBLK + jnp.arange(TBLK, dtype=jnp.int32)
    row_perms = jnp.argsort(col_scores, axis=2).astype(jnp.int32)
    row_ends = jnp.cumsum(counts, axis=1).astype(jnp.int32)
    starts = row_ends - counts
    slot_ids = jnp.arange(KCAP, dtype=jnp.int32)
    slot_rows = jnp.sum((row_ends[:, None, :] <= slot_ids[None, :, None]).astype(jnp.int32), axis=2).astype(jnp.int32)
    slot_rows = jnp.minimum(slot_rows, TBLK - 1)
    freq_ids = jnp.arange(F, dtype=jnp.int32)[:, None]
    within = (slot_ids[None, :] - starts[freq_ids, slot_rows]) % TBLK
    columns = row_perms[freq_ids, slot_rows, within]
    return (counts.astype(jnp.int32), columns.astype(jnp.int32))


def draw_row_counts(key, part):
    return tile_layout(key)[0]


def draw_tile_cols(key, part):
    return tile_layout(key)[1]


def block_scale(own_key, dims, pieces, low, high):
    def one(dim, shards_of):
        heights = jax.random.uniform(jax.random.fold_in(jax.random.fold_in(own_key, 6), dim), (shards_of,), jnp.float32, low / len(pieces), high / len(pieces))
        return jnp.repeat(jnp.exp(heights), dims[dim] // shards_of).reshape((-1,) + (1,) * (len(dims) - dim - 1))

    factor_of = one(*pieces[0])
    for cut in pieces[1:]:
        factor_of = factor_of * one(*cut)
    return factor_of


def bell_draw(rng, shape, scale, bound, cuts=(), kind=jnp.bfloat16):
    gain = block_scale(rng, shape, cuts, -0.22, 0.18) if cuts else 1.0
    drawn = jax.random.normal(rng, shape, jnp.float32) * scale * gain
    return jnp.minimum(jnp.maximum(drawn, -bound), bound).astype(kind)


def setup_inputs(seed: int = 0, part: int = 0) -> dict:
    key_of = jax.random.split(jax.random.key(seed), 5)
    part_keys = jax.random.split(jax.random.fold_in(key_of[4], part), 5)
    traces = bell_draw(part_keys[0], (NT, R, V), 1.0, 6.0, ((1, 8), (2, 2)))
    row_counts = draw_row_counts(jax.random.fold_in(jax.random.fold_in(key_of[4], part), 71), part)
    tile_cols = draw_tile_cols(jax.random.fold_in(jax.random.fold_in(key_of[4], part), 71), part)
    tiles = bell_draw(part_keys[3], (F, KCAP, 2, TILE, TILE), (10 * TILE) ** -0.5, 0.15625, ((0, 8), (1, 2)))
    return dict(traces=traces, row_counts=row_counts, tile_cols=tile_cols, tiles=tiles)


def transform_tables(samples, frequencies):
    sample_ids = jnp.arange(samples, dtype=jnp.int32)
    freq_ids = 1 + jnp.arange(frequencies, dtype=jnp.int32)
    turn_index = (freq_ids[:, None] * sample_ids[None, :]) % samples
    phases = turn_index.astype(jnp.float32) * (2.0 * math.pi / samples)
    norm_scale = samples ** -0.5
    cosine = jnp.cos(phases)
    sine_part = jnp.sin(phases)
    forward = (jnp.stack([cosine, -sine_part], axis=1) * norm_scale).astype(jnp.bfloat16)
    inverse = (jnp.stack([cosine, -sine_part], axis=2) * (2.0 * norm_scale)).transpose(1, 0, 2).astype(jnp.bfloat16)
    return forward, inverse


def to_bfloat(value):
    return lax.optimization_barrier(value.astype(jnp.bfloat16)).astype(jnp.float32)


def row_weights(row_ends, slot_ids, row_total):
    slot_rows = jnp.sum((row_ends[None, :] <= slot_ids[:, None]).astype(jnp.int32), axis=1).astype(jnp.int32)
    alive = slot_ids < row_ends[-1]
    slot_rows = jnp.minimum(slot_rows, row_total - 1)
    match = (slot_rows[:, None] == jnp.arange(row_total, dtype=jnp.int32)[None, :]) & alive[:, None]
    return match.astype(jnp.float32)


def half_partial(spectrum, counts, columns, kernel, first_id):
    slot_count = kernel.shape[0]
    tile_size = kernel.shape[-1]
    row_ends = jnp.cumsum(counts).astype(jnp.int32)
    slot_ids = (first_id + jnp.arange(slot_count, dtype=jnp.int32)).astype(jnp.int32)
    weights = row_weights(row_ends, slot_ids, counts.shape[0])
    blocks = spectrum.reshape(-1, tile_size, 2, spectrum.shape[-1])
    picked = jnp.take(blocks, columns, axis=0)
    products = jnp.einsum('kcij,kjdv->kcidv', kernel.astype(jnp.float32), picked.astype(jnp.float32))
    real_part = products[:, 0, :, 0] - products[:, 1, :, 1]
    imag_part = products[:, 0, :, 1] + products[:, 1, :, 0]
    slot_terms = jnp.stack([real_part, imag_part], axis=2)
    summed = jnp.einsum('kr,kxcv->rxcv', weights, slot_terms)
    return summed.reshape(spectrum.shape)


def reference(traces, row_counts, tile_cols, tiles):
    forward, inverse = transform_tables(NT, F)
    spectra = jnp.einsum('fct,trv->frcv', forward.astype(jnp.float32), traces.astype(jnp.float32)).astype(jnp.bfloat16)

    def one_frequency(item):
        spectrum, counts, columns, kernel = item
        lower = half_partial(spectrum, counts, columns[:KHALF], kernel[:KHALF], 0)
        upper = half_partial(spectrum, counts, columns[KHALF:], kernel[KHALF:], KHALF)
        return (to_bfloat(lower) + to_bfloat(upper)).astype(jnp.bfloat16)

    redatumed = lax.map(one_frequency, (spectra, row_counts, tile_cols, tiles))
    result = jnp.einsum('tfc,frcv->trv', inverse.astype(jnp.float32), redatumed.astype(jnp.float32))
    return result.astype(jnp.bfloat16)
```

```python
import functools
import math

import jax
import jax.numpy as jnp
import numpy as np
from jax import lax
from jax.experimental import pallas as pl
from jax.experimental.pallas import tpu as pltpu
from jax.sharding import PartitionSpec as P

BF16 = jnp.bfloat16
F32 = jnp.float32
SUB = 16


def transform_tables(samples, frequencies):
    turns = (1 + np.arange(frequencies))[:, None] * np.arange(samples)[None, :] % samples
    phases = turns * (2.0 * math.pi / samples)
    both = np.stack([np.cos(phases), -np.sin(phases)], axis=1) * samples**-0.5
    small = both.astype(jnp.bfloat16)
    twice = (2.0 * both).astype(jnp.bfloat16)
    forward = np.zeros((frequencies, 2, SUB, samples, SUB), jnp.bfloat16)
    inverse = np.zeros((samples, SUB, frequencies, 2, SUB), jnp.bfloat16)
    for r in range(SUB):
        forward[:, :, r, :, r] = small
        inverse[:, r, :, :, r] = twice.transpose(2, 0, 1)
    return (
        forward.reshape(frequencies, 2 * SUB, samples * SUB),
        inverse.reshape(samples * SUB, frequencies * 2 * SUB),
    )


def params(**kwargs):
    return pltpu.CompilerParams(vmem_limit_bytes=56 * 2**20, **kwargs)


def forward_kernel(group, blocks, me_ref, table_ref, traces_ref, *out_refs):
    samples, _, width = traces_ref.shape
    me = me_ref[0]
    columns = jnp.concatenate(
        [
            traces_ref[:, SUB * b : SUB * (b + 1), :].reshape(samples * SUB, width)
            for b in range(blocks)
        ],
        axis=1,
    )
    for first in range(0, len(out_refs), group):
        table = jnp.concatenate([table_ref[me ^ s] for s in range(first, first + group)], axis=0)
        found = jnp.dot(table, columns, preferred_element_type=F32).astype(BF16)
        for s in range(group):
            for c in range(2):
                for b in range(blocks):
                    row = (2 * s + c) * SUB
                    out_refs[first + s][c, SUB * b : SUB * (b + 1), :] = found[
                        row : row + SUB, width * b : width * (b + 1)
                    ]


def forward(me, table, traces, first, count):
    samples, _, width = traces.shape
    parties = table.shape[0]
    step = min(2 * SUB, count)
    return pl.pallas_call(
        functools.partial(forward_kernel, min(8, parties), step // SUB),
        grid_spec=pltpu.PrefetchScalarGridSpec(
            num_scalar_prefetch=1,
            grid=(count // step,),
            in_specs=[
                pl.BlockSpec(table.shape, lambda i, _: (0, 0, 0), pipeline_mode=pl.Buffered(1)),
                pl.BlockSpec((samples, step, width), lambda i, _: (0, first // step + i, 0)),
            ],
            out_specs=[pl.BlockSpec((2, step, width), lambda i, _: (0, i, 0))] * parties,
        ),
        out_shape=[jax.ShapeDtypeStruct((2, count, width), BF16)] * parties,
        compiler_params=params(),
        cost_estimate=pl.CostEstimate(
            flops=2 * parties * 32 * samples * SUB * width * count // SUB,
            bytes_accessed=2 * samples * count * width,
            transcendentals=0,
        ),
        name="forward",
    )(me, table, traces)


def tiles_kernel(parties, taken, given, slot_ref, own_ref, other_ref, *refs):
    in_refs = refs[: parties * len(taken)]
    out_refs = refs[parties * len(taken) : parties * (len(taken) + len(given))]
    top_ref, low_ref, sum_ref = refs[-3:]
    step = pl.program_id(0)
    block, _, size, _ = own_ref.shape
    width = in_refs[0].shape[-1]
    rows = sum(count for _, count in taken)
    me = slot_ref[2, 0]

    @pl.when(step == 0)
    def _():
        for q, (first, count) in enumerate(taken):
            for s in range(parties):
                ref = in_refs[q * parties + s]
                place = pl.ds(pl.multiple_of((me ^ s) * rows + first, SUB), count)
                top_ref[place, :width] = ref[0]
                top_ref[place, width:] = ref[1]
                low_ref[place, :width] = -ref[1]
                low_ref[place, width:] = ref[0]
        sum_ref[...] = jnp.zeros_like(sum_ref)

    for k in range(block):
        for which, ref in ((0, own_ref), (1, other_ref)):
            slot = step * block + k
            target = slot_ref[which, slot]
            column = slot_ref[3 + which, slot]
            place = pl.ds(pl.multiple_of(column * size, size), size)
            pair = jnp.concatenate([ref[k, 0], ref[k, 1]], axis=1)
            weights = jnp.concatenate([top_ref[place, :], low_ref[place, :]], axis=0)
            spot = pl.ds(pl.multiple_of(target * size, size), size)
            sum_ref[spot, :] += jnp.dot(pair, weights, preferred_element_type=F32)

    @pl.when(step == pl.num_programs(0) - 1)
    def _():
        for q, (first, count) in enumerate(given):
            for s in range(parties):
                place = pl.ds(pl.multiple_of((me ^ s) * rows + first, SUB), count)
                ref = out_refs[q * parties + s]
                ref[0] = sum_ref[place, :width].astype(BF16)
                ref[1] = sum_ref[place, width:].astype(BF16)


def apply_tiles(slots, own, other, spectra, taken, given):
    parties = len(spectra) // len(taken)
    halves, _, size, _ = own.shape
    width = spectra[0].shape[-1]
    total = parties * sum(count for _, count in taken)
    block = math.gcd(8, halves)
    whole = lambda i, _: (0, 0, 0)
    return pl.pallas_call(
        functools.partial(tiles_kernel, parties, taken, given),
        grid_spec=pltpu.PrefetchScalarGridSpec(
            num_scalar_prefetch=1,
            grid=(halves // block,),
            in_specs=[pl.BlockSpec((block, 2, size, size), lambda i, _: (i, 0, 0, 0))] * 2
            + [pl.BlockSpec(a.shape, whole, pipeline_mode=pl.Buffered(1)) for a in spectra],
            out_specs=[
                pl.BlockSpec((2, count, width), whole)
                for _, count in given
                for _ in range(parties)
            ],
            scratch_shapes=[
                pltpu.VMEM((total, 2 * width), BF16),
                pltpu.VMEM((total, 2 * width), BF16),
                pltpu.VMEM((total + size, 2 * width), F32),
            ],
        ),
        out_shape=[
            jax.ShapeDtypeStruct((2, count, width), BF16)
            for _, count in given
            for _ in range(parties)
        ],
        compiler_params=params(),
        cost_estimate=pl.CostEstimate(
            flops=2 * 2 * halves * size * 4 * size * width,
            bytes_accessed=4 * own.size,
            transcendentals=0,
        ),
        name="tiles",
    )(slots, own, other, *spectra)


def inverse_kernel(parties, blocks, me_ref, table_ref, *refs):
    in_refs = refs[:parties]
    out_ref, held_ref = refs[-2:]
    samples, _, width = out_ref.shape
    me = me_ref[0]

    @pl.when(pl.program_id(1) == 0)
    def _():
        for s in range(parties):
            for c in range(2):
                for b in range(blocks):
                    held_ref[me ^ s, SUB * c : SUB * (c + 1), width * b : width * (b + 1)] = (
                        in_refs[s][c, SUB * b : SUB * (b + 1), :]
                    )

    found = jnp.dot(
        table_ref[...],
        held_ref[...].reshape(parties * 2 * SUB, blocks * width),
        preferred_element_type=F32,
    ).astype(BF16)
    for b in range(blocks):
        out_ref[:, SUB * b : SUB * (b + 1), :] = found[:, width * b : width * (b + 1)].reshape(
            samples, SUB, width
        )


def inverse(me, table, redatumed, first, rows, filled):
    parties = len(redatumed)
    _, count, width = redatumed[0].shape
    samples = table.shape[0] // SUB
    step = min(2 * SUB, count)
    parts = 4
    extra = [] if filled is None else [filled]

    def kernel(me_ref, table_ref, *refs):
        refs = refs if filled is None else refs[:parties] + refs[parties + 1 :]
        inverse_kernel(parties, step // SUB, me_ref, table_ref, *refs)

    return pl.pallas_call(
        kernel,
        grid_spec=pltpu.PrefetchScalarGridSpec(
            num_scalar_prefetch=1,
            grid=(count // step, parts),
            in_specs=[pl.BlockSpec((samples // parts * SUB, table.shape[1]), lambda i, j, _: (j, 0))]
            + [pl.BlockSpec((2, step, width), lambda i, j, _: (0, i, 0))] * parties
            + [pl.BlockSpec(memory_space=pl.ANY)] * len(extra),
            out_specs=pl.BlockSpec(
                (samples // parts, step, width), lambda i, j, _: (j, first // step + i, 0)
            ),
            scratch_shapes=[pltpu.VMEM((parties, 2 * SUB, step // SUB * width), BF16)],
        ),
        out_shape=jax.ShapeDtypeStruct((samples, rows, width), BF16),
        input_output_aliases={} if filled is None else {2 + parties: 0},
        compiler_params=params(),
        cost_estimate=pl.CostEstimate(
            flops=2 * parties * 32 * samples * SUB * width * count // SUB,
            bytes_accessed=2 * samples * count * width,
            transcendentals=0,
        ),
        name="inverse",
    )(me, table, *redatumed, *extra)


def exchange(blocks):
    parties = len(blocks)
    got = [blocks[0]]
    for s in range(1, parties):
        pairs = [(k, k ^ s) for k in range(parties)]
        got.append(lax.ppermute(blocks[s], "wide", pairs))
    return got


def cuts(rows, sizes):
    if rows % (sum(sizes) * 2 * SUB):
        return ((0, rows),)
    unit = rows // sum(sizes)
    return tuple((unit * sum(sizes[:i]), unit * n) for i, n in enumerate(sizes))


def shards(traces, row_counts, tile_cols, tiles):
    samples, rows, _ = traces.shape
    parties = lax.axis_size("wide")
    halves = tiles.shape[1]
    forward_table, inverse_table = transform_tables(samples, parties)
    me = lax.axis_index("wide").astype(jnp.int32)
    side = lax.axis_index("narrow").astype(jnp.int32)
    taken = cuts(rows, (1, 3))
    given = cuts(rows, (3, 1))

    other = lax.ppermute(tiles[0], "narrow", [(0, 1), (1, 0)])
    ends = jnp.cumsum(row_counts[0])
    slot_ids = jnp.arange(2 * halves, dtype=jnp.int32)
    slot_rows = jnp.sum((ends[None, :] <= slot_ids[:, None]).astype(jnp.int32), axis=1)
    columns = jnp.clip(tile_cols[0], 0, row_counts.shape[1] - 1)
    turn = lambda a: jnp.where(side == 0, a.reshape(2, halves), a.reshape(2, halves)[::-1])
    slots = jnp.concatenate(
        [turn(slot_rows), jnp.full((1, halves), me, jnp.int32), turn(columns)], axis=0
    )

    place = me.reshape(1)
    spectra = []
    for first, count in taken:
        spectra += exchange(forward(place, forward_table, traces, first, count))
    redatumed = apply_tiles(slots, tiles[0], other, spectra, taken, given)
    result = None
    for q, (first, _) in enumerate(given):
        blocks = exchange(redatumed[q * parties : (q + 1) * parties])
        result = inverse(place, inverse_table, blocks, first, rows, result)
    return result


def solution(mesh):
    in_specs = (
        P(None, ("groups", "wide"), "narrow"),
        P(("groups", "wide"), None),
        P(("groups", "wide"), None),
        P(("groups", "wide"), "narrow", None, None, None),
    )
    out_specs = P(None, ("groups", "wide"), "narrow")
    return jax.shard_map(shards, mesh=mesh, in_specs=in_specs, out_specs=out_specs, check_vma=False)
```

```python
import functools
import math

import jax
import jax.numpy as jnp
import numpy as np
from jax import lax
from jax.experimental import pallas as pl
from jax.experimental.pallas import tpu as pltpu
from jax.sharding import PartitionSpec as P

BF16 = jnp.bfloat16
F32 = jnp.float32
SUB = 16
LANES = 128
CUTS = (1, 1)


def transform_tables(samples, frequencies):
    turns = (1 + np.arange(frequencies))[:, None] * np.arange(samples)[None, :] % samples
    phases = turns * (2.0 * math.pi / samples)
    both = np.stack([np.cos(phases), -np.sin(phases)], axis=1) * samples**-0.5
    small = both.astype(jnp.bfloat16)
    twice = (2.0 * both).astype(jnp.bfloat16)
    forward = np.zeros((frequencies, 2, SUB, samples, SUB), jnp.bfloat16)
    inverse = np.zeros((samples, SUB, frequencies, 2, SUB), jnp.bfloat16)
    for r in range(SUB):
        forward[:, :, r, :, r] = small
        inverse[:, r, :, :, r] = twice.transpose(2, 0, 1)

    def cut(table):
        high, wide = table.shape
        return np.ascontiguousarray(table.reshape(high, wide // LANES, LANES).transpose(1, 0, 2))

    return (
        cut(forward.reshape(frequencies * 2 * SUB, samples * SUB)),
        cut(inverse.reshape(samples * SUB, frequencies * 2 * SUB)),
    )


def params():
    return pltpu.CompilerParams(vmem_limit_bytes=52 * 2**20)


def place_of(me, s, rows, first, count):
    return pl.ds(pl.multiple_of((me ^ s) * rows + first, SUB), count)


def forward_kernel(first, step, early, sends, me_ref, table_hbm, traces_hbm, *refs):
    early_ref = refs[0] if early else None
    out_refs = refs[1 if early else 0 : -4]
    table_ref, traces_ref, table_sem, sems = refs[-4:]
    steps, samples, _, width = traces_ref.shape
    tiles, high, _ = table_ref.shape
    part = min(256, high)
    me = me_ref[0]

    def fetch(i):
        return pltpu.make_async_copy(
            traces_hbm.at[:, pl.ds(first + i * step, step), :], traces_ref.at[i], sems.at[i]
        )

    table_copy = pltpu.make_async_copy(table_hbm, table_ref, table_sem)
    table_copy.start()
    for i in range(steps):
        fetch(i).start()
    if early:
        for s in range(early):
            out_refs[s][:, :first, :] = early_ref[s]
    table_copy.wait()

    @pl.loop(0, steps)
    def _(i):
        fetch(i).wait()
        columns = jnp.concatenate(
            [
                traces_ref[i, :, b : b + SUB, :].reshape(samples * SUB, width)
                for b in range(0, step, SUB)
            ],
            axis=1,
        )
        for low in range(0, high, part):
            group = range(low // (2 * SUB), (low + part) // (2 * SUB))
            table = jnp.concatenate(
                [
                    jnp.concatenate(
                        [table_ref[k, place_of(me, s, 2 * SUB, 0, 2 * SUB), :] for s in group],
                        axis=0,
                    )
                    for k in range(tiles)
                ],
                axis=1,
            )
            found = jnp.dot(table, columns, preferred_element_type=F32).astype(BF16)
            for s in group:
                ref, lead, begin = sends[s]
                for c in range(2):
                    row = (2 * s + c) * SUB - low
                    for b in range(step // SUB):
                        spot = pl.ds(pl.multiple_of(begin + i * step + b * SUB, SUB), SUB)
                        out_refs[ref][lead + (c, spot, slice(None))] = found[
                            row : row + SUB, width * b : width * (b + 1)
                        ]


def forward(me, table, traces, first, count, shapes, sends, early):
    samples, _, width = traces.shape
    step = min(2 * SUB, count)
    extra = [] if early is None else [early]
    return pl.pallas_call(
        functools.partial(forward_kernel, first, step, 0 if early is None else early.shape[0], sends),
        in_specs=[pl.BlockSpec(memory_space=pltpu.SMEM)]
        + [pl.BlockSpec(memory_space=pl.ANY)] * 2
        + [pl.BlockSpec(memory_space=pltpu.VMEM)] * len(extra),
        out_specs=[pl.BlockSpec(memory_space=pltpu.VMEM)] * len(shapes),
        scratch_shapes=[
            pltpu.VMEM(table.shape, BF16),
            pltpu.VMEM((count // step, samples, step, width), BF16),
            pltpu.SemaphoreType.DMA,
            pltpu.SemaphoreType.DMA((count // step,)),
        ],
        out_shape=[jax.ShapeDtypeStruct(shape, BF16) for shape in shapes],
        compiler_params=params(),
        cost_estimate=pl.CostEstimate(
            flops=table.shape[1] * 2 * samples * width * count,
            bytes_accessed=2 * samples * count * width,
            transcendentals=0,
        ),
        name="forward",
    )(me, table, traces, *extra)


def tiles_kernel(rows, messages, block, slot_ref, me_ref, own_hbm, other_hbm, *refs):
    in_refs = refs[: len(messages)]
    out_refs = refs[len(messages) : 2 * len(messages)]
    tile_ref, top_ref, low_ref, sum_ref, sems = refs[-5:]
    _, halves, _, size, _ = tile_ref.shape
    width = in_refs[0].shape[-1]
    steps = halves // block
    me = me_ref[0]

    def fetch(which, q):
        source = (own_hbm, other_hbm)[which]
        part = pl.ds(q * block, block)
        return pltpu.make_async_copy(source.at[part], tile_ref.at[which, part], sems.at[which, q])

    for q in range(steps):
        for which in range(2):
            fetch(which, q).start()

    for ref, (s, first, count) in zip(in_refs, messages):
        place = place_of(me, s, rows, first, count)
        top_ref[place, :width] = ref[0]
        top_ref[place, width:] = ref[1]
        low_ref[place, :width] = -ref[1]
        low_ref[place, width:] = ref[0]
    sum_ref[...] = jnp.zeros_like(sum_ref)

    @pl.loop(0, steps)
    def _(q):
        for which in range(2):
            fetch(which, q).wait()
        for k in range(block):
            for which in range(2):
                slot = q * block + k
                column = slot_ref[2 + which, slot]
                place = pl.ds(pl.multiple_of(column * size, size), size)
                pair = jnp.concatenate(
                    [tile_ref[which, slot, 0], tile_ref[which, slot, 1]], axis=1
                )
                weights = jnp.concatenate([top_ref[place, :], low_ref[place, :]], axis=0)
                spot = pl.ds(pl.multiple_of(slot_ref[which, slot] * size, size), size)
                sum_ref[spot, :] += jnp.dot(pair, weights, preferred_element_type=F32)

    for ref, (s, first, count) in zip(out_refs, messages):
        place = place_of(me, s, rows, first, count)
        ref[0] = sum_ref[place, :width].astype(BF16)
        ref[1] = sum_ref[place, width:].astype(BF16)


def apply_tiles(slots, me, own, other, rows, messages, spectra):
    halves, _, size, _ = own.shape
    width = spectra[0].shape[-1]
    total = sum(count for _, _, count in messages)
    block = math.gcd(8, halves)
    return pl.pallas_call(
        functools.partial(tiles_kernel, rows, messages, block),
        in_specs=[pl.BlockSpec(memory_space=pltpu.SMEM)] * 2
        + [pl.BlockSpec(memory_space=pl.ANY)] * 2
        + [pl.BlockSpec(memory_space=pltpu.VMEM)] * len(messages),
        out_specs=[pl.BlockSpec(memory_space=pltpu.VMEM)] * len(messages),
        scratch_shapes=[
            pltpu.VMEM((2,) + own.shape, BF16),
            pltpu.VMEM((total, 2 * width), BF16),
            pltpu.VMEM((total, 2 * width), BF16),
            pltpu.VMEM((total + size, 2 * width), F32),
            pltpu.SemaphoreType.DMA((2, halves // block)),
        ],
        out_shape=[jax.ShapeDtypeStruct((2, count, width), BF16) for _, _, count in messages],
        compiler_params=params(),
        cost_estimate=pl.CostEstimate(
            flops=2 * 2 * halves * size * 4 * size * width,
            bytes_accessed=4 * own.size,
            transcendentals=0,
        ),
        name="tiles",
    )(slots, me, own, other, *spectra)


def inverse_kernel(first, step, offsets, me_ref, table_ref, *refs):
    parties = len(offsets)
    in_refs = refs[:parties]
    out_hbm, column_ref, held_ref, sems = refs[-4:]
    steps, samples, _, width = held_ref.shape
    part = min(4096, samples * SUB)
    me = me_ref[0]

    def send(i):
        return pltpu.make_async_copy(
            held_ref.at[i], out_hbm.at[:, pl.ds(first + i * step, step), :], sems.at[i]
        )

    @pl.loop(0, steps)
    def _(i):
        for s in range(parties):
            for c in range(2):
                for b in range(step // SUB):
                    spot = pl.ds(pl.multiple_of(offsets[s] + i * step + b * SUB, SUB), SUB)
                    column_ref[
                        place_of(me, s, 2 * SUB, c * SUB, SUB), width * b : width * (b + 1)
                    ] = in_refs[s][c, spot, :]
        for low in range(0, samples * SUB, part):
            table = jnp.concatenate(
                [table_ref[k, low : low + part, :] for k in range(table_ref.shape[0])], axis=1
            )
            found = jnp.dot(table, column_ref[...], preferred_element_type=F32).astype(BF16)
            for b in range(step // SUB):
                held_ref[i, low // SUB : (low + part) // SUB, SUB * b : SUB * (b + 1), :] = found[
                    :, width * b : width * (b + 1)
                ].reshape(part // SUB, SUB, width)
        send(i).start()

    for i in range(steps):
        send(i).wait()


def inverse(me, table, blocks, offsets, first, count, rows, filled):
    width = blocks[0].shape[-1]
    samples = table.shape[1] // SUB
    step = min(2 * SUB, count)
    extra = [] if filled is None else [filled]
    return pl.pallas_call(
        functools.partial(inverse_kernel, first, step, offsets),
        in_specs=[pl.BlockSpec(memory_space=pltpu.SMEM)]
        + [pl.BlockSpec(memory_space=pltpu.VMEM)] * (1 + len(blocks))
        + [pl.BlockSpec(memory_space=pl.ANY)] * len(extra),
        out_specs=pl.BlockSpec(memory_space=pl.ANY),
        scratch_shapes=[
            pltpu.VMEM((len(blocks) * 2 * SUB, step // SUB * width), BF16),
            pltpu.VMEM((count // step, samples, step, width), BF16),
            pltpu.SemaphoreType.DMA((count // step,)),
        ],
        out_shape=jax.ShapeDtypeStruct((samples, rows, width), BF16),
        input_output_aliases={2 + len(blocks): 0} if extra else {},
        compiler_params=params(),
        cost_estimate=pl.CostEstimate(
            flops=len(blocks) * 4 * SUB * samples * width * count,
            bytes_accessed=2 * samples * count * width,
            transcendentals=0,
        ),
        name="inverse",
    )(me, table, *blocks, *extra)


def send(block, s, parties):
    if s == 0:
        return block
    return lax.ppermute(block, "wide", [(k, k ^ s) for k in range(parties)])


def cuts(rows, sizes):
    if rows % (sum(sizes) * 2 * SUB):
        return ((0, rows),)
    unit = rows // sum(sizes)
    return tuple((unit * sum(sizes[:i]), unit * n) for i, n in enumerate(sizes))


def shards(traces, row_counts, tile_cols, tiles):
    samples, rows, width = traces.shape
    parties = lax.axis_size("wide")
    halves = tiles.shape[1]
    forward_table, inverse_table = transform_tables(samples, parties)
    side = lax.axis_index("narrow").astype(jnp.int32)
    me = lax.axis_index("wide").astype(jnp.int32).reshape(1)
    chunks = cuts(rows, CUTS)
    near = parties // 2
    whole = [(s, 0, rows) for s in range(near)]
    far = [[(s, first, count) for s in range(near, parties)] for first, count in chunks]
    messages = [m for part in far for m in part] + whole[::-1]

    other = lax.ppermute(tiles[0], "narrow", [(0, 1), (1, 0)])
    ends = jnp.cumsum(row_counts[0])
    slot_ids = jnp.arange(2 * halves, dtype=jnp.int32)
    slot_rows = jnp.sum((ends[None, :] <= slot_ids[:, None]).astype(jnp.int32), axis=1)
    columns = jnp.clip(tile_cols[0], 0, row_counts.shape[1] - 1)
    turn = lambda a: jnp.where(side == 0, a.reshape(2, halves), a.reshape(2, halves)[::-1])
    slots = jnp.concatenate([turn(slot_rows), turn(columns)], axis=0)

    got = {}
    early = None
    for q, (first, count) in enumerate(chunks):
        last = q == len(chunks) - 1
        shapes = [(2, rows, width)] * near if last else [(near, 2, first + count, width)]
        sends = [(s, (), first) if last else (0, (s,), first) for s in range(near)]
        sends += [(len(shapes) + k, (), 0) for k in range(parties - near)]
        shapes += [(2, count, width)] * (parties - near)
        found = forward(me, forward_table, traces, first, count, shapes, sends, early)
        early = None if last else found[0]
        for m, block in zip(far[q], found[-(parties - near) :]):
            got[m] = send(block, m[0], parties)
        if last:
            for m, block in list(zip(whole, found))[::-1]:
                got[m] = send(block, m[0], parties)

    found = apply_tiles(slots, me, tiles[0], other, rows, messages, [got[m] for m in messages])
    got = {m: send(block, m[0], parties) for m, block in zip(messages, found)}
    result = None
    for (first, count), part in zip(chunks, far):
        blocks = [got[m] for m in whole + part]
        offsets = [first] * near + [0] * (parties - near)
        result = inverse(me, inverse_table, blocks, offsets, first, count, rows, result)
    return result


def solution(mesh):
    in_specs = (
        P(None, ("groups", "wide"), "narrow"),
        P(("groups", "wide"), None),
        P(("groups", "wide"), None),
        P(("groups", "wide"), "narrow", None, None, None),
    )
    out_specs = P(None, ("groups", "wide"), "narrow")
    return jax.shard_map(shards, mesh=mesh, in_specs=in_specs, out_specs=out_specs, check_vma=False)
```

```python
import functools
import math

import jax
import jax.numpy as jnp
import numpy as np
from jax import lax
from jax.experimental import pallas as pl
from jax.experimental.pallas import tpu as pltpu
from jax.sharding import PartitionSpec as P

BF16 = jnp.bfloat16
F32 = jnp.float32
SUB = 16
LANES = 128
MAXROW = 8
CUTS = (1, 1)


def transform_tables(samples, frequencies):
    turns = (1 + np.arange(frequencies))[:, None] * np.arange(samples)[None, :] % samples
    phases = turns * (2.0 * math.pi / samples)
    both = np.stack([np.cos(phases), -np.sin(phases)], axis=1) * samples**-0.5
    small = both.astype(jnp.bfloat16)
    twice = (2.0 * both).astype(jnp.bfloat16)
    forward = np.zeros((frequencies, 2, SUB, samples, SUB), jnp.bfloat16)
    inverse = np.zeros((samples, SUB, frequencies, 2, SUB), jnp.bfloat16)
    for r in range(SUB):
        forward[:, :, r, :, r] = small
        inverse[:, r, :, :, r] = twice.transpose(2, 0, 1)

    def cut(table):
        high, wide = table.shape
        return np.ascontiguousarray(table.reshape(high, wide // LANES, LANES).transpose(1, 0, 2))

    return (
        cut(forward.reshape(frequencies * 2 * SUB, samples * SUB)),
        cut(inverse.reshape(samples * SUB, frequencies * 2 * SUB)),
    )


def params(limit):
    return pltpu.CompilerParams(vmem_limit_bytes=min(limit, 56 * 2**20))


def place_of(me, k, rows, first, count):
    return pl.ds(pl.multiple_of((me ^ k) * rows + first, SUB), count)


def forward_kernel(first, step, me_ref, table_hbm, traces_hbm, *refs):
    early_refs = refs[:1] if first else ()
    near_ref, *far_refs = refs[len(early_refs) : -4]
    near = near_ref.shape[0]
    table_ref, traces_ref, table_sem, sems = refs[-4:]
    steps, samples, _, width = traces_ref.shape
    tiles, high, _ = table_ref.shape
    part = min(256, high)
    me = me_ref[0]

    def fetch(i):
        return pltpu.make_async_copy(
            traces_hbm.at[:, pl.ds(first + i * step, step), :], traces_ref.at[i], sems.at[i]
        )

    table_copy = pltpu.make_async_copy(table_hbm, table_ref, table_sem)
    table_copy.start()
    for i in range(steps):
        fetch(i).start()
    for ref in early_refs:
        near_ref[:, :, :first, :] = ref[...]
    table_copy.wait()

    @pl.loop(0, steps)
    def _(i):
        fetch(i).wait()
        columns = jnp.concatenate(
            [
                traces_ref[i, :, b : b + SUB, :].reshape(samples * SUB, width)
                for b in range(0, step, SUB)
            ],
            axis=1,
        )
        for low in range(0, high, part):
            group = range(low // (2 * SUB), (low + part) // (2 * SUB))
            table = jnp.concatenate(
                [
                    jnp.concatenate(
                        [table_ref[k, place_of(me, s, 2 * SUB, 0, 2 * SUB), :] for s in group],
                        axis=0,
                    )
                    for k in range(tiles)
                ],
                axis=1,
            )
            found = jnp.dot(table, columns, preferred_element_type=F32).astype(BF16)
            for s in group:
                ref, begin = (near_ref.at[s], first) if s < near else (far_refs[s - near], 0)
                for c in range(2):
                    row = (2 * s + c) * SUB - low
                    for b in range(step // SUB):
                        spot = pl.ds(pl.multiple_of(begin + i * step + b * SUB, SUB), SUB)
                        ref[c, spot, :] = found[row : row + SUB, width * b : width * (b + 1)]


def forward(me, table, traces, near, first, count, early):
    samples, _, width = traces.shape
    parties = table.shape[1] // (2 * SUB)
    step = min(2 * SUB, count)
    extra = [early] if first else []
    shapes = [(near, 2, first + count, width)] + [(2, count, width)] * (parties - near)
    return pl.pallas_call(
        functools.partial(forward_kernel, first, step),
        in_specs=[pl.BlockSpec(memory_space=pltpu.SMEM)]
        + [pl.BlockSpec(memory_space=pl.ANY)] * 2
        + [pl.BlockSpec(memory_space=pltpu.VMEM)] * len(extra),
        out_specs=[pl.BlockSpec(memory_space=pltpu.VMEM)] * len(shapes),
        scratch_shapes=[
            pltpu.VMEM(table.shape, BF16),
            pltpu.VMEM((count // step, samples, step, width), BF16),
            pltpu.SemaphoreType.DMA,
            pltpu.SemaphoreType.DMA((count // step,)),
        ],
        out_shape=[jax.ShapeDtypeStruct(shape, BF16) for shape in shapes],
        compiler_params=params(50 * 2**20),
        cost_estimate=pl.CostEstimate(
            flops=table.shape[1] * 2 * samples * width * count,
            bytes_accessed=2 * samples * count * width,
            transcendentals=0,
        ),
        name="forward",
    )(me, table, traces, *extra)


def tiles_kernel(near, chunks, block, count_ref, column_ref, place_ref, own_hbm, other_hbm, *refs):
    rows, width = refs[0].shape[1:]
    far = refs[-7].shape[0] if len(chunks) > 1 else (len(refs) - 6) // 2 - near
    ins = near + far * len(chunks)
    near_in, far_in = refs[:near], refs[near:ins]
    near_out, far_out = refs[ins : ins + near], refs[ins + near : -6]
    tile_ref, top_ref, low_ref, sum_ref, row_ref, sems = refs[-6:]
    _, halves, _, size, _ = tile_ref.shape
    steps = halves // block
    me, side = place_ref[0], place_ref[1]
    tile_rows = count_ref.shape[1]

    def fetch(which, q):
        source = (own_hbm, other_hbm)[which]
        part = pl.ds(q * block, block)
        return pltpu.make_async_copy(source.at[part], tile_ref.at[which, part], sems.at[which, q])

    for q in range(steps):
        for which in range(2):
            fetch(which, q).start()

    for slot in range(2 * halves):
        row_ref[slot] = tile_rows
    begin = jnp.int32(0)
    for row in range(tile_rows + 1):
        for k in range(MAXROW):
            row_ref[begin + k] = row
        begin += count_ref[0, row] if row < tile_rows else 0

    def take(k, first, count, ref):
        place = place_of(me, k, rows, first, count)
        top_ref[place, :width] = ref[0]
        top_ref[place, width:] = ref[1]
        low_ref[place, :width] = -ref[1]
        low_ref[place, width:] = ref[0]

    def give(k, first, count, ref):
        place = place_of(me, k, rows, first, count)
        ref[0] = sum_ref[place, :width].astype(BF16)
        ref[1] = sum_ref[place, width:].astype(BF16)

    for k in range(near):
        take(k, 0, rows, near_in[k])
    for q, (first, count) in enumerate(chunks):
        for j in range(far):
            take(near + j, first, count, far_in[q * far + j])
    sum_ref[...] = jnp.zeros_like(sum_ref)

    @pl.loop(0, steps)
    def _(q):
        for which in range(2):
            fetch(which, q).wait()
        for k in range(block):
            for which in range(2):
                slot = q * block + k
                own = (side ^ which) * halves + slot
                column = jnp.clip(column_ref[0, own], 0, tile_rows - 1)
                place = pl.ds(pl.multiple_of(column * size, size), size)
                pair = jnp.concatenate(
                    [tile_ref[which, slot, 0], tile_ref[which, slot, 1]], axis=1
                )
                weights = jnp.concatenate([top_ref[place, :], low_ref[place, :]], axis=0)
                spot = pl.ds(pl.multiple_of(row_ref[own] * size, size), size)
                sum_ref[spot, :] += jnp.dot(pair, weights, preferred_element_type=F32)

    for k in range(near):
        give(k, 0, rows, near_out[k])
    for j in range(far):
        give(near + j, *chunks[0], far_out[j])
    for ref in far_out[far:]:
        for j in range(far):
            give(near + j, *chunks[1], ref.at[j])


def apply_tiles(counts, columns, place, own, other, chunks, nears, fars):
    halves, _, size, _ = own.shape
    _, rows, width = nears[0].shape
    far = len(fars) // len(chunks)
    total = (len(nears) + far) * rows
    block = math.gcd(8, halves)
    shapes = [nears[0].shape] * len(nears) + [(2, chunks[0][1], width)] * far
    shapes += [(far, 2, part, width) for _, part in chunks[1:]]
    return pl.pallas_call(
        functools.partial(tiles_kernel, len(nears), chunks, block),
        in_specs=[pl.BlockSpec(memory_space=pltpu.SMEM)] * 3
        + [pl.BlockSpec(memory_space=pl.ANY)] * 2
        + [pl.BlockSpec(memory_space=pltpu.VMEM)] * (len(nears) + len(fars)),
        out_specs=[pl.BlockSpec(memory_space=pltpu.VMEM)] * len(shapes),
        scratch_shapes=[
            pltpu.VMEM((2,) + own.shape, BF16),
            pltpu.VMEM((total, 2 * width), BF16),
            pltpu.VMEM((total, 2 * width), BF16),
            pltpu.VMEM((total + size, 2 * width), F32),
            pltpu.SMEM((2 * halves + MAXROW,), jnp.int32),
            pltpu.SemaphoreType.DMA((2, halves // block)),
        ],
        out_shape=[jax.ShapeDtypeStruct(shape, BF16) for shape in shapes],
        compiler_params=params(50 * 2**20),
        cost_estimate=pl.CostEstimate(
            flops=2 * 2 * halves * size * 4 * size * width,
            bytes_accessed=4 * own.size,
            transcendentals=0,
        ),
        name="tiles",
    )(counts, columns, place, own, other, *nears, *fars)


def split_kernel(in_ref, *out_refs):
    for j, ref in enumerate(out_refs):
        ref[...] = in_ref[j]


def split(late):
    return pl.pallas_call(
        split_kernel,
        in_specs=[pl.BlockSpec(memory_space=pltpu.VMEM)],
        out_specs=[pl.BlockSpec(memory_space=pltpu.VMEM)] * late.shape[0],
        out_shape=[jax.ShapeDtypeStruct(late.shape[1:], BF16)] * late.shape[0],
        compiler_params=params(50 * 2**20),
        cost_estimate=pl.CostEstimate(flops=0, bytes_accessed=1 << 24, transcendentals=0),
        name="split",
    )(late)


def inverse_kernel(first, step, parties, near, me_ref, table_ref, *refs):
    in_refs = refs[:parties]
    out_hbm, column_ref, held_ref, sems = refs[-4:]
    steps, samples, _, width = held_ref.shape
    part = min(4096, samples * SUB)
    me = me_ref[0]

    def send(i):
        return pltpu.make_async_copy(
            held_ref.at[i], out_hbm.at[:, pl.ds(first + i * step, step), :], sems.at[i]
        )

    @pl.loop(0, steps)
    def _(i):
        for s in range(parties):
            for c in range(2):
                for b in range(step // SUB):
                    ref, begin = in_refs[s], first if s < near else 0
                    spot = pl.ds(pl.multiple_of(begin + i * step + b * SUB, SUB), SUB)
                    column_ref[
                        place_of(me, s, 2 * SUB, c * SUB, SUB), width * b : width * (b + 1)
                    ] = ref[c, spot, :]
        for low in range(0, samples * SUB, part):
            table = jnp.concatenate(
                [table_ref[k, low : low + part, :] for k in range(table_ref.shape[0])], axis=1
            )
            found = jnp.dot(table, column_ref[...], preferred_element_type=F32).astype(BF16)
            for b in range(step // SUB):
                held_ref[i, low // SUB : (low + part) // SUB, SUB * b : SUB * (b + 1), :] = found[
                    :, width * b : width * (b + 1)
                ].reshape(part // SUB, SUB, width)
        send(i).start()

    for i in range(steps):
        send(i).wait()


def inverse(me, table, nears, fars, first, count, filled):
    _, rows, width = nears[0].shape
    parties = len(nears) + len(fars)
    samples = table.shape[1] // SUB
    step = min(2 * SUB, count)
    extra = [] if filled is None else [filled]
    return pl.pallas_call(
        functools.partial(inverse_kernel, first, step, parties, len(nears)),
        in_specs=[pl.BlockSpec(memory_space=pltpu.SMEM)]
        + [pl.BlockSpec(memory_space=pltpu.VMEM)] * (1 + parties)
        + [pl.BlockSpec(memory_space=pl.ANY)] * len(extra),
        out_specs=pl.BlockSpec(memory_space=pl.ANY),
        scratch_shapes=[
            pltpu.VMEM((parties * 2 * SUB, step // SUB * width), BF16),
            pltpu.VMEM((count // step, samples, step, width), BF16),
            pltpu.SemaphoreType.DMA((count // step,)),
        ],
        out_shape=jax.ShapeDtypeStruct((samples, rows, width), BF16),
        input_output_aliases={2 + parties: 0} if extra else {},
        compiler_params=params(
            2 * samples * (SUB * LANES * table.shape[0] * 5 // 4 + count * width) + 14 * 2**20
        ),
        cost_estimate=pl.CostEstimate(
            flops=parties * 4 * SUB * samples * width * count,
            bytes_accessed=2 * samples * count * width,
            transcendentals=0,
        ),
        name="inverse",
    )(me, table, *nears, *fars, *extra)


def send(block, k, parties):
    return lax.ppermute(block, "wide", [(i, i ^ k) for i in range(parties)]) if k else block


def cuts(rows, sizes):
    if rows % (sum(sizes) * 2 * SUB):
        return ((0, rows),)
    unit = rows // sum(sizes)
    return tuple((unit * sum(sizes[:i]), unit * n) for i, n in enumerate(sizes))


def shards(traces, row_counts, tile_cols, tiles):
    samples, rows, _ = traces.shape
    parties = lax.axis_size("wide")
    forward_table, inverse_table = transform_tables(samples, parties)
    me = jnp.stack([lax.axis_index("wide"), lax.axis_index("narrow")]).astype(jnp.int32)
    chunks = cuts(rows, CUTS)
    near = parties // 2
    far = range(near, parties)

    early = None
    got = []
    for first, count in chunks:
        early, *blocks = forward(me, forward_table, traces, near, first, count, early)
        if not first:
            own_tiles, early = lax.optimization_barrier((tiles[0], early))
        got += [send(block, k, parties) for k, block in zip(far, blocks)]
    other = lax.ppermute(own_tiles, "narrow", [(0, 1), (1, 0)])
    other, early = lax.optimization_barrier((other, early))
    nears = [send(block, k, parties) for k, block in enumerate(split(early))]

    sums = apply_tiles(row_counts, tile_cols, me, own_tiles, other, chunks, nears, got)
    nears, blocks, late = sums[:near], sums[near:parties], sums[parties:]
    got = [[send(block, k, parties) for k, block in zip(far, blocks)]]
    nears = [send(block, k, parties) for k, block in enumerate(nears)]
    for blocks in late:
        got.append([send(block, k, parties) for k, block in zip(far, split(blocks))])
    result = None
    for (first, count), blocks in zip(chunks, got):
        result = inverse(me, inverse_table, nears, blocks, first, count, result)
    return result


def solution(mesh):
    in_specs = (
        P(None, ("groups", "wide"), "narrow"),
        P(("groups", "wide"), None),
        P(("groups", "wide"), None),
        P(("groups", "wide"), "narrow", None, None, None),
    )
    out_specs = P(None, ("groups", "wide"), "narrow")
    return jax.shard_map(shards, mesh=mesh, in_specs=in_specs, out_specs=out_specs, check_vma=False)
```

```python
import functools
import math

import jax
import jax.numpy as jnp
import numpy as np
from jax import lax
from jax.experimental import pallas as pl
from jax.experimental.pallas import tpu as pltpu
from jax.sharding import PartitionSpec as P

BF16 = jnp.bfloat16
F32 = jnp.float32
SUB = 16
LANES = 128
MAXROW = 8
CUTS = (1, 1)


def even_terms(samples):
    return -(-(samples // 2 + 1) * SUB // LANES) * LANES // SUB


def transform_tables(samples, frequencies):
    turns = (1 + np.arange(frequencies))[:, None] * np.arange(samples)[None, :] % samples
    phases = turns * (2.0 * math.pi / samples)
    both = np.stack([np.cos(phases), -np.sin(phases)], axis=1) * samples**-0.5
    small = both.astype(jnp.bfloat16)
    twice = (2.0 * both).astype(jnp.bfloat16)
    half = samples // 2
    even = np.zeros((frequencies, SUB, even_terms(samples), SUB), jnp.bfloat16)
    odd = np.zeros((frequencies, SUB, half, SUB), jnp.bfloat16)
    inverse = np.zeros((samples, SUB, frequencies, 2, SUB), jnp.bfloat16)
    for r in range(SUB):
        even[:, r, : half + 1, r] = small[:, 0, : half + 1]
        odd[:, r, 1:, r] = small[:, 1, 1:half]
        inverse[:, r, :, :, r] = twice.transpose(2, 0, 1)

    def cut(table, high):
        table = table.reshape(high, -1, LANES)
        return np.ascontiguousarray(table.transpose(1, 0, 2))

    forward = np.concatenate([cut(even, frequencies * SUB), cut(odd, frequencies * SUB)])
    return forward, cut(inverse, samples * SUB)


def params(limit):
    return pltpu.CompilerParams(vmem_limit_bytes=min(limit, 56 * 2**20))


def place_of(me, k, rows, first, count):
    return pl.ds(pl.multiple_of((me ^ k) * rows + first, SUB), count)


def forward_kernel(first, step, me_ref, table_hbm, traces_hbm, *refs):
    early_refs = refs[:1] if first else ()
    near_ref, *far_refs = refs[len(early_refs) : -4]
    near = near_ref.shape[0]
    table_ref, traces_ref, table_sem, sems = refs[-4:]
    steps, samples, _, width = traces_ref.shape
    tiles, high, _ = table_ref.shape
    part = min(128, high)
    me = me_ref[0]

    def fetch(i):
        return pltpu.make_async_copy(
            traces_hbm.at[:, pl.ds(first + i * step, step), :], traces_ref.at[i], sems.at[i]
        )

    table_copy = pltpu.make_async_copy(table_hbm, table_ref, table_sem)
    table_copy.start()
    for i in range(steps):
        fetch(i).start()
    for ref in early_refs:
        near_ref[:, :, :first, :] = ref[...]
    table_copy.wait()

    @pl.loop(0, steps)
    def _(i):
        fetch(i).wait()

        def sample(t, b):
            return traces_ref[i, t, b : b + SUB, :]

        def even(t, b):
            if t in (0, half):
                return sample(t, b)
            return sample(t, b) + sample(samples - t, b) if t < half else empty

        def odd(t, b):
            return sample(t, b) - sample(samples - t, b) if t else empty

        half = samples // 2
        empty = jnp.zeros((SUB, width), BF16)
        cosines = even_terms(samples) * SUB // LANES
        for c, (fold, terms, pieces) in enumerate(
            (
                (even, even_terms(samples), range(cosines)),
                (odd, half, range(cosines, tiles)),
            )
        ):
            columns = jnp.concatenate(
                [
                    jnp.concatenate([fold(t, b) for t in range(terms)], axis=0)
                    for b in range(0, step, SUB)
                ],
                axis=1,
            )
            for low in range(0, high, part):
                group = range(low // SUB, (low + part) // SUB)
                table = jnp.concatenate(
                    [
                        jnp.concatenate(
                            [table_ref[k, place_of(me, s, SUB, 0, SUB), :] for s in group], axis=0
                        )
                        for k in pieces
                    ],
                    axis=1,
                )
                found = jnp.dot(table, columns, preferred_element_type=F32).astype(BF16)
                for s in group:
                    ref, begin = (near_ref.at[s], first) if s < near else (far_refs[s - near], 0)
                    row = s * SUB - low
                    for b in range(step // SUB):
                        spot = pl.ds(pl.multiple_of(begin + i * step + b * SUB, SUB), SUB)
                        ref[c, spot, :] = found[row : row + SUB, width * b : width * (b + 1)]


def forward(me, table, traces, near, first, count, early):
    samples, _, width = traces.shape
    parties = table.shape[1] // SUB
    step = min(2 * SUB, count)
    extra = [early] if first else []
    shapes = [(near, 2, first + count, width)] + [(2, count, width)] * (parties - near)
    return pl.pallas_call(
        functools.partial(forward_kernel, first, step),
        in_specs=[pl.BlockSpec(memory_space=pltpu.SMEM)]
        + [pl.BlockSpec(memory_space=pl.ANY)] * 2
        + [pl.BlockSpec(memory_space=pltpu.VMEM)] * len(extra),
        out_specs=[pl.BlockSpec(memory_space=pltpu.VMEM)] * len(shapes),
        scratch_shapes=[
            pltpu.VMEM(table.shape, BF16),
            pltpu.VMEM((count // step, samples, step, width), BF16),
            pltpu.SemaphoreType.DMA,
            pltpu.SemaphoreType.DMA((count // step,)),
        ],
        out_shape=[jax.ShapeDtypeStruct(shape, BF16) for shape in shapes],
        compiler_params=params(52 * 2**20),
        cost_estimate=pl.CostEstimate(
            flops=table.shape[1] * 4 * samples * width * count,
            bytes_accessed=2 * samples * count * width,
            transcendentals=0,
        ),
        name="forward",
    )(me, table, traces, *extra)


def tiles_kernel(near, chunks, block, count_ref, column_ref, place_ref, own_hbm, other_hbm, *refs):
    rows, width = refs[0].shape[1:]
    far = refs[-7].shape[0] if len(chunks) > 1 else (len(refs) - 6) // 2 - near
    ins = near + far * len(chunks)
    near_in, far_in = refs[:near], refs[near:ins]
    near_out, far_out = refs[ins : ins + near], refs[ins + near : -6]
    tile_ref, top_ref, low_ref, sum_ref, row_ref, sems = refs[-6:]
    _, halves, _, size, _ = tile_ref.shape
    steps = halves // block
    me, side = place_ref[0], place_ref[1]
    tile_rows = count_ref.shape[1]

    def fetch(which, q):
        source = (own_hbm, other_hbm)[which]
        part = pl.ds(q * block, block)
        return pltpu.make_async_copy(source.at[part], tile_ref.at[which, part], sems.at[which, q])

    for q in range(steps):
        for which in range(2):
            fetch(which, q).start()

    for slot in range(2 * halves):
        row_ref[slot] = tile_rows
    begin = jnp.int32(0)
    for row in range(tile_rows + 1):
        for k in range(MAXROW):
            row_ref[begin + k] = row
        begin += count_ref[0, row] if row < tile_rows else 0

    def take(k, first, count, ref):
        place = place_of(me, k, rows, first, count)
        top_ref[place, :width] = ref[0]
        top_ref[place, width:] = ref[1]
        low_ref[place, :width] = -ref[1]
        low_ref[place, width:] = ref[0]

    def give(k, first, count, ref):
        place = place_of(me, k, rows, first, count)
        ref[0] = sum_ref[place, :width].astype(BF16)
        ref[1] = sum_ref[place, width:].astype(BF16)

    for k in range(near):
        take(k, 0, rows, near_in[k])
    for q, (first, count) in enumerate(chunks):
        for j in range(far):
            take(near + j, first, count, far_in[q * far + j])
    sum_ref[...] = jnp.zeros_like(sum_ref)

    @pl.loop(0, steps)
    def _(q):
        for which in range(2):
            fetch(which, q).wait()
        for k in range(block):
            for which in range(2):
                slot = q * block + k
                own = (side ^ which) * halves + slot
                column = jnp.clip(column_ref[0, own], 0, tile_rows - 1)
                place = pl.ds(pl.multiple_of(column * size, size), size)
                pair = jnp.concatenate(
                    [tile_ref[which, slot, 0], tile_ref[which, slot, 1]], axis=1
                )
                weights = jnp.concatenate([top_ref[place, :], low_ref[place, :]], axis=0)
                spot = pl.ds(pl.multiple_of(row_ref[own] * size, size), size)
                sum_ref[spot, :] += jnp.dot(pair, weights, preferred_element_type=F32)

    for k in range(near):
        give(k, 0, rows, near_out[k])
    for j in range(far):
        give(near + j, *chunks[0], far_out[j])
    for ref in far_out[far:]:
        for j in range(far):
            give(near + j, *chunks[1], ref.at[j])


def apply_tiles(counts, columns, place, own, other, chunks, nears, fars):
    halves, _, size, _ = own.shape
    _, rows, width = nears[0].shape
    far = len(fars) // len(chunks)
    total = (len(nears) + far) * rows
    block = math.gcd(8, halves)
    shapes = [nears[0].shape] * len(nears) + [(2, chunks[0][1], width)] * far
    shapes += [(far, 2, part, width) for _, part in chunks[1:]]
    return pl.pallas_call(
        functools.partial(tiles_kernel, len(nears), chunks, block),
        in_specs=[pl.BlockSpec(memory_space=pltpu.SMEM)] * 3
        + [pl.BlockSpec(memory_space=pl.ANY)] * 2
        + [pl.BlockSpec(memory_space=pltpu.VMEM)] * (len(nears) + len(fars)),
        out_specs=[pl.BlockSpec(memory_space=pltpu.VMEM)] * len(shapes),
        scratch_shapes=[
            pltpu.VMEM((2,) + own.shape, BF16),
            pltpu.VMEM((total, 2 * width), BF16),
            pltpu.VMEM((total, 2 * width), BF16),
            pltpu.VMEM((total + size, 2 * width), F32),
            pltpu.SMEM((2 * halves + MAXROW,), jnp.int32),
            pltpu.SemaphoreType.DMA((2, halves // block)),
        ],
        out_shape=[jax.ShapeDtypeStruct(shape, BF16) for shape in shapes],
        compiler_params=params(28 * 2**20),
        cost_estimate=pl.CostEstimate(
            flops=2 * 2 * halves * size * 4 * size * width,
            bytes_accessed=4 * own.size,
            transcendentals=0,
        ),
        name="tiles",
    )(counts, columns, place, own, other, *nears, *fars)


def split_kernel(in_ref, *out_refs):
    for j, ref in enumerate(out_refs):
        ref[...] = in_ref[j]


def split(late):
    return pl.pallas_call(
        split_kernel,
        in_specs=[pl.BlockSpec(memory_space=pltpu.VMEM)],
        out_specs=[pl.BlockSpec(memory_space=pltpu.VMEM)] * late.shape[0],
        out_shape=[jax.ShapeDtypeStruct(late.shape[1:], BF16)] * late.shape[0],
        compiler_params=params(50 * 2**20),
        cost_estimate=pl.CostEstimate(flops=0, bytes_accessed=1 << 24, transcendentals=0),
        name="split",
    )(late)


def inverse_kernel(first, step, parties, near, me_ref, table_ref, *refs):
    in_refs = refs[:parties]
    out_hbm, column_ref, held_ref, sems = refs[-4:]
    steps, samples, _, width = held_ref.shape
    part = min(4096, samples * SUB)
    me = me_ref[0]

    def send(i):
        return pltpu.make_async_copy(
            held_ref.at[i], out_hbm.at[:, pl.ds(first + i * step, step), :], sems.at[i]
        )

    @pl.loop(0, steps)
    def _(i):
        for s in range(parties):
            for c in range(2):
                for b in range(step // SUB):
                    ref, begin = in_refs[s], first if s < near else 0
                    spot = pl.ds(pl.multiple_of(begin + i * step + b * SUB, SUB), SUB)
                    column_ref[
                        place_of(me, s, 2 * SUB, c * SUB, SUB), width * b : width * (b + 1)
                    ] = ref[c, spot, :]
        for low in range(0, samples * SUB, part):
            table = jnp.concatenate(
                [table_ref[k, low : low + part, :] for k in range(table_ref.shape[0])], axis=1
            )
            found = jnp.dot(table, column_ref[...], preferred_element_type=F32).astype(BF16)
            for b in range(step // SUB):
                held_ref[i, low // SUB : (low + part) // SUB, SUB * b : SUB * (b + 1), :] = found[
                    :, width * b : width * (b + 1)
                ].reshape(part // SUB, SUB, width)
        send(i).start()

    for i in range(steps):
        send(i).wait()


def inverse(me, table, nears, fars, first, count, filled):
    _, rows, width = nears[0].shape
    parties = len(nears) + len(fars)
    samples = table.shape[1] // SUB
    step = min(2 * SUB, count)
    extra = [] if filled is None else [filled]
    return pl.pallas_call(
        functools.partial(inverse_kernel, first, step, parties, len(nears)),
        in_specs=[pl.BlockSpec(memory_space=pltpu.SMEM)]
        + [pl.BlockSpec(memory_space=pltpu.VMEM)] * (1 + parties)
        + [pl.BlockSpec(memory_space=pl.ANY)] * len(extra),
        out_specs=pl.BlockSpec(memory_space=pl.ANY),
        scratch_shapes=[
            pltpu.VMEM((parties * 2 * SUB, step // SUB * width), BF16),
            pltpu.VMEM((count // step, samples, step, width), BF16),
            pltpu.SemaphoreType.DMA((count // step,)),
        ],
        out_shape=jax.ShapeDtypeStruct((samples, rows, width), BF16),
        input_output_aliases={2 + parties: 0} if extra else {},
        compiler_params=params(
            2 * samples * (SUB * LANES * table.shape[0] * 5 // 4 + count * width) + 14 * 2**20
        ),
        cost_estimate=pl.CostEstimate(
            flops=parties * 4 * SUB * samples * width * count,
            bytes_accessed=2 * samples * count * width,
            transcendentals=0,
        ),
        name="inverse",
    )(me, table, *nears, *fars, *extra)


def send(block, k, parties):
    return lax.ppermute(block, "wide", [(i, i ^ k) for i in range(parties)]) if k else block


def cuts(rows, sizes):
    if rows % (sum(sizes) * 2 * SUB):
        return ((0, rows),)
    unit = rows // sum(sizes)
    return tuple((unit * sum(sizes[:i]), unit * n) for i, n in enumerate(sizes))


def shards(traces, row_counts, tile_cols, tiles):
    samples, rows, _ = traces.shape
    parties = lax.axis_size("wide")
    forward_table, inverse_table = transform_tables(samples, parties)
    me = jnp.stack([lax.axis_index("wide"), lax.axis_index("narrow")]).astype(jnp.int32)
    chunks = cuts(rows, CUTS)
    near = parties // 2
    far = range(near, parties)

    early = None
    got = []
    for first, count in chunks:
        early, *blocks = forward(me, forward_table, traces, near, first, count, early)
        got += [send(block, k, parties) for k, block in zip(far, blocks)]
    other = lax.ppermute(tiles[0], "narrow", [(0, 1), (1, 0)])
    other, early = lax.optimization_barrier((other, early))
    nears = [send(block, k, parties) for k, block in enumerate(split(early))]

    sums = apply_tiles(row_counts, tile_cols, me, tiles[0], other, chunks, nears, got)
    nears, blocks, late = sums[:near], sums[near:parties], sums[parties:]
    got = [[send(block, k, parties) for k, block in zip(far, blocks)]]
    nears = [send(block, k, parties) for k, block in enumerate(nears)]
    for blocks in late:
        got.append([send(block, k, parties) for k, block in zip(far, split(blocks))])
    result = None
    for (first, count), blocks in zip(chunks, got):
        result = inverse(me, inverse_table, nears, blocks, first, count, result)
    return result


def solution(mesh):
    in_specs = (
        P(None, ("groups", "wide"), "narrow"),
        P(("groups", "wide"), None),
        P(("groups", "wide"), None),
        P(("groups", "wide"), "narrow", None, None, None),
    )
    out_specs = P(None, ("groups", "wide"), "narrow")
    return jax.shard_map(shards, mesh=mesh, in_specs=in_specs, out_specs=out_specs, check_vma=False)
```

```python
import functools
import math

import jax
import jax.numpy as jnp
import numpy as np
from jax import lax
from jax.experimental import pallas as pl
from jax.experimental.pallas import tpu as pltpu
from jax.sharding import PartitionSpec as P

BF16 = jnp.bfloat16
F32 = jnp.float32
SUB = 16
LANES = 128
MAXROW = 8
CUTS = (1, 1)


def even_terms(samples):
    return -(-(samples // 2 + 1) * SUB // LANES) * LANES // SUB


def transform_tables(samples, frequencies):
    turns = (1 + np.arange(frequencies))[:, None] * np.arange(samples)[None, :] % samples
    phases = turns * (2.0 * math.pi / samples)
    both = np.stack([np.cos(phases), -np.sin(phases)], axis=1) * samples**-0.5
    small = both.astype(jnp.bfloat16)
    twice = (2.0 * both).astype(jnp.bfloat16)
    half = samples // 2
    even = np.zeros((frequencies, SUB, even_terms(samples), SUB), jnp.bfloat16)
    odd = np.zeros((frequencies, SUB, half, SUB), jnp.bfloat16)
    inverse = np.zeros((samples, SUB, frequencies, 2, SUB), jnp.bfloat16)
    for r in range(SUB):
        even[:, r, : half + 1, r] = small[:, 0, : half + 1]
        odd[:, r, 1:, r] = small[:, 1, 1:half]
        inverse[:, r, :, :, r] = twice.transpose(2, 0, 1)

    def cut(table, high):
        table = table.reshape(high, -1, LANES)
        return np.ascontiguousarray(table.transpose(1, 0, 2))

    forward = np.concatenate([cut(even, frequencies * SUB), cut(odd, frequencies * SUB)])
    return forward, cut(inverse, samples * SUB)


def params(limit):
    return pltpu.CompilerParams(vmem_limit_bytes=min(limit, 56 * 2**20))


def place_of(me, k, rows, first, count):
    return pl.ds(pl.multiple_of((me ^ k) * rows + first, SUB), count)


def forward_kernel(first, step, me_ref, table_hbm, traces_hbm, *refs):
    early_refs = refs[:1] if first else ()
    near_ref, *far_refs = refs[len(early_refs) : -4]
    near = near_ref.shape[0]
    table_ref, traces_ref, table_sem, sems = refs[-4:]
    steps, samples, _, width = traces_ref.shape
    tiles, high, _ = table_ref.shape
    part = min(128, high)
    me = me_ref[0]

    def fetch(i):
        return pltpu.make_async_copy(
            traces_hbm.at[:, pl.ds(first + i * step, step), :], traces_ref.at[i], sems.at[i]
        )

    table_copy = pltpu.make_async_copy(table_hbm, table_ref, table_sem)
    table_copy.start()
    for i in range(steps):
        fetch(i).start()
    for ref in early_refs:
        near_ref[:, :, :first, :] = ref[...]
    table_copy.wait()

    @pl.loop(0, steps)
    def _(i):
        fetch(i).wait()

        def sample(t, b):
            return traces_ref[i, t, b : b + SUB, :]

        def even(t, b):
            if t in (0, half):
                return sample(t, b)
            return sample(t, b) + sample(samples - t, b) if t < half else empty

        def odd(t, b):
            return sample(t, b) - sample(samples - t, b) if t else empty

        half = samples // 2
        empty = jnp.zeros((SUB, width), BF16)
        cosines = even_terms(samples) * SUB // LANES
        for c, (fold, terms, pieces) in enumerate(
            (
                (even, even_terms(samples), range(cosines)),
                (odd, half, range(cosines, tiles)),
            )
        ):
            columns = jnp.concatenate(
                [
                    jnp.concatenate([fold(t, b) for t in range(terms)], axis=0)
                    for b in range(0, step, SUB)
                ],
                axis=1,
            )
            for low in range(0, high, part):
                group = range(low // SUB, (low + part) // SUB)
                table = jnp.concatenate(
                    [
                        jnp.concatenate(
                            [table_ref[k, place_of(me, s, SUB, 0, SUB), :] for s in group], axis=0
                        )
                        for k in pieces
                    ],
                    axis=1,
                )
                found = jnp.dot(table, columns, preferred_element_type=F32).astype(BF16)
                for s in group:
                    ref, begin = (near_ref.at[s], first) if s < near else (far_refs[s - near], 0)
                    row = s * SUB - low
                    for b in range(step // SUB):
                        spot = pl.ds(pl.multiple_of(begin + i * step + b * SUB, SUB), SUB)
                        ref[c, spot, :] = found[row : row + SUB, width * b : width * (b + 1)]


def forward(me, table, traces, near, first, count, early):
    samples, _, width = traces.shape
    parties = table.shape[1] // SUB
    step = min(2 * SUB, count)
    extra = [early] if first else []
    shapes = [(near, 2, first + count, width)] + [(2, count, width)] * (parties - near)
    return pl.pallas_call(
        functools.partial(forward_kernel, first, step),
        in_specs=[pl.BlockSpec(memory_space=pltpu.SMEM)]
        + [pl.BlockSpec(memory_space=pl.ANY)] * 2
        + [pl.BlockSpec(memory_space=pltpu.VMEM)] * len(extra),
        out_specs=[pl.BlockSpec(memory_space=pltpu.VMEM)] * len(shapes),
        scratch_shapes=[
            pltpu.VMEM(table.shape, BF16),
            pltpu.VMEM((count // step, samples, step, width), BF16),
            pltpu.SemaphoreType.DMA,
            pltpu.SemaphoreType.DMA((count // step,)),
        ],
        out_shape=[jax.ShapeDtypeStruct(shape, BF16) for shape in shapes],
        compiler_params=params(52 * 2**20),
        cost_estimate=pl.CostEstimate(
            flops=table.shape[1] * 4 * samples * width * count,
            bytes_accessed=2 * samples * count * width,
            transcendentals=0,
        ),
        name="forward",
    )(me, table, traces, *extra)


def tiles_kernel(near, chunks, block, count_ref, column_ref, place_ref, own_hbm, other_hbm, *refs):
    rows, width = refs[0].shape[1:]
    far = refs[-7].shape[0] if len(chunks) > 1 else (len(refs) - 6) // 2 - near
    ins = near + far * len(chunks)
    near_in, far_in = refs[:near], refs[near:ins]
    near_out, far_out = refs[ins : ins + near], refs[ins + near : -6]
    tile_ref, top_ref, low_ref, sum_ref, row_ref, sems = refs[-6:]
    _, halves, _, size, _ = tile_ref.shape
    steps = halves // block
    me, side = place_ref[0], place_ref[1]
    tile_rows = count_ref.shape[1]

    def fetch(which, q):
        source = (own_hbm, other_hbm)[which]
        part = pl.ds(q * block, block)
        return pltpu.make_async_copy(source.at[part], tile_ref.at[which, part], sems.at[which, q])

    for q in range(steps):
        for which in range(2):
            fetch(which, q).start()

    for slot in range(2 * halves):
        row_ref[slot] = tile_rows
    begin = jnp.int32(0)
    for row in range(tile_rows + 1):
        for k in range(MAXROW):
            row_ref[begin + k] = row
        begin += count_ref[0, row] if row < tile_rows else 0

    def take(k, first, count, ref):
        place = place_of(me, k, rows, first, count)
        top_ref[place, :width] = ref[0]
        top_ref[place, width:] = ref[1]
        low_ref[place, :width] = -ref[1]
        low_ref[place, width:] = ref[0]

    def give(k, first, count, ref):
        place = place_of(me, k, rows, first, count)
        ref[0] = sum_ref[place, :width].astype(BF16)
        ref[1] = sum_ref[place, width:].astype(BF16)

    for k in range(near):
        take(k, 0, rows, near_in[k])
    for q, (first, count) in enumerate(chunks):
        for j in range(far):
            take(near + j, first, count, far_in[q * far + j])
    sum_ref[...] = jnp.zeros_like(sum_ref)

    @pl.loop(0, steps)
    def _(q):
        for which in range(2):
            fetch(which, q).wait()
        for k in range(block):
            for which in range(2):
                slot = q * block + k
                own = (side ^ which) * halves + slot
                column = jnp.clip(column_ref[0, own], 0, tile_rows - 1)
                place = pl.ds(pl.multiple_of(column * size, size), size)
                pair = jnp.concatenate(
                    [tile_ref[which, slot, 0], tile_ref[which, slot, 1]], axis=1
                )
                weights = jnp.concatenate([top_ref[place, :], low_ref[place, :]], axis=0)
                spot = pl.ds(pl.multiple_of(row_ref[own] * size, size), size)
                sum_ref[spot, :] += jnp.dot(pair, weights, preferred_element_type=F32)

    for k in range(near):
        give(k, 0, rows, near_out[k])
    for j in range(far):
        give(near + j, *chunks[0], far_out[j])
    for ref in far_out[far:]:
        for j in range(far):
            give(near + j, *chunks[1], ref.at[j])


def apply_tiles(counts, columns, place, own, other, chunks, nears, fars):
    halves, _, size, _ = own.shape
    _, rows, width = nears[0].shape
    far = len(fars) // len(chunks)
    total = (len(nears) + far) * rows
    block = math.gcd(20, halves)
    shapes = [nears[0].shape] * len(nears) + [(2, chunks[0][1], width)] * far
    shapes += [(far, 2, part, width) for _, part in chunks[1:]]
    return pl.pallas_call(
        functools.partial(tiles_kernel, len(nears), chunks, block),
        in_specs=[pl.BlockSpec(memory_space=pltpu.SMEM)] * 3
        + [pl.BlockSpec(memory_space=pl.ANY)] * 2
        + [pl.BlockSpec(memory_space=pltpu.VMEM)] * (len(nears) + len(fars)),
        out_specs=[pl.BlockSpec(memory_space=pltpu.VMEM)] * len(shapes),
        scratch_shapes=[
            pltpu.VMEM((2,) + own.shape, BF16),
            pltpu.VMEM((total, 2 * width), BF16),
            pltpu.VMEM((total, 2 * width), BF16),
            pltpu.VMEM((total + size, 2 * width), F32),
            pltpu.SMEM((2 * halves + MAXROW,), jnp.int32),
            pltpu.SemaphoreType.DMA((2, halves // block)),
        ],
        out_shape=[jax.ShapeDtypeStruct(shape, BF16) for shape in shapes],
        compiler_params=params(28 * 2**20),
        cost_estimate=pl.CostEstimate(
            flops=2 * 2 * halves * size * 4 * size * width,
            bytes_accessed=4 * own.size,
            transcendentals=0,
        ),
        name="tiles",
    )(counts, columns, place, own, other, *nears, *fars)


def split_kernel(in_ref, *out_refs):
    for j, ref in enumerate(out_refs):
        ref[...] = in_ref[j]


def split(late):
    return pl.pallas_call(
        split_kernel,
        in_specs=[pl.BlockSpec(memory_space=pltpu.VMEM)],
        out_specs=[pl.BlockSpec(memory_space=pltpu.VMEM)] * late.shape[0],
        out_shape=[jax.ShapeDtypeStruct(late.shape[1:], BF16)] * late.shape[0],
        compiler_params=params(50 * 2**20),
        cost_estimate=pl.CostEstimate(flops=0, bytes_accessed=1 << 24, transcendentals=0),
        name="split",
    )(late)


def inverse_kernel(first, step, parties, near, me_ref, table_ref, *refs):
    in_refs = refs[:parties]
    out_hbm, column_ref, held_ref, sems = refs[-4:]
    steps, samples, _, width = held_ref.shape
    part = min(4096, samples * SUB)
    me = me_ref[0]

    def send(i):
        return pltpu.make_async_copy(
            held_ref.at[i], out_hbm.at[:, pl.ds(first + i * step, step), :], sems.at[i]
        )

    @pl.loop(0, steps)
    def _(i):
        for s in range(parties):
            for c in range(2):
                for b in range(step // SUB):
                    ref, begin = in_refs[s], first if s < near else 0
                    spot = pl.ds(pl.multiple_of(begin + i * step + b * SUB, SUB), SUB)
                    column_ref[
                        place_of(me, s, 2 * SUB, c * SUB, SUB), width * b : width * (b + 1)
                    ] = ref[c, spot, :]
        for low in range(0, samples * SUB, part):
            table = jnp.concatenate(
                [table_ref[k, low : low + part, :] for k in range(table_ref.shape[0])], axis=1
            )
            found = jnp.dot(table, column_ref[...], preferred_element_type=F32).astype(BF16)
            for b in range(step // SUB):
                held_ref[i, low // SUB : (low + part) // SUB, SUB * b : SUB * (b + 1), :] = found[
                    :, width * b : width * (b + 1)
                ].reshape(part // SUB, SUB, width)
        send(i).start()

    for i in range(steps):
        send(i).wait()


def inverse(me, table, nears, fars, first, count, filled):
    _, rows, width = nears[0].shape
    parties = len(nears) + len(fars)
    samples = table.shape[1] // SUB
    step = min(2 * SUB, count)
    extra = [] if filled is None else [filled]
    return pl.pallas_call(
        functools.partial(inverse_kernel, first, step, parties, len(nears)),
        in_specs=[pl.BlockSpec(memory_space=pltpu.SMEM)]
        + [pl.BlockSpec(memory_space=pltpu.VMEM)] * (1 + parties)
        + [pl.BlockSpec(memory_space=pl.ANY)] * len(extra),
        out_specs=pl.BlockSpec(memory_space=pl.ANY),
        scratch_shapes=[
            pltpu.VMEM((parties * 2 * SUB, step // SUB * width), BF16),
            pltpu.VMEM((count // step, samples, step, width), BF16),
            pltpu.SemaphoreType.DMA((count // step,)),
        ],
        out_shape=jax.ShapeDtypeStruct((samples, rows, width), BF16),
        input_output_aliases={2 + parties: 0} if extra else {},
        compiler_params=params(
            2 * samples * (SUB * LANES * table.shape[0] * 5 // 4 + count * width) + 14 * 2**20
        ),
        cost_estimate=pl.CostEstimate(
            flops=parties * 4 * SUB * samples * width * count,
            bytes_accessed=2 * samples * count * width,
            transcendentals=0,
        ),
        name="inverse",
    )(me, table, *nears, *fars, *extra)


def send(block, k, parties):
    return lax.ppermute(block, "wide", [(i, i ^ k) for i in range(parties)]) if k else block


def cuts(rows, sizes):
    if rows % (sum(sizes) * 2 * SUB):
        return ((0, rows),)
    unit = rows // sum(sizes)
    return tuple((unit * sum(sizes[:i]), unit * n) for i, n in enumerate(sizes))


def shards(traces, row_counts, tile_cols, tiles):
    samples, rows, _ = traces.shape
    parties = lax.axis_size("wide")
    forward_table, inverse_table = transform_tables(samples, parties)
    me = jnp.stack([lax.axis_index("wide"), lax.axis_index("narrow")]).astype(jnp.int32)
    chunks = cuts(rows, CUTS)
    near = parties // 2
    far = range(near, parties)

    early = None
    got = []
    for first, count in chunks:
        early, *blocks = forward(me, forward_table, traces, near, first, count, early)
        got += [send(block, k, parties) for k, block in zip(far, blocks)]
    other = lax.ppermute(tiles[0], "narrow", [(0, 1), (1, 0)])
    other, early = lax.optimization_barrier((other, early))
    nears = [send(block, k, parties) for k, block in enumerate(split(early))]

    sums = apply_tiles(row_counts, tile_cols, me, tiles[0], other, chunks, nears, got)
    nears, blocks, late = sums[:near], sums[near:parties], sums[parties:]
    got = [[send(block, k, parties) for k, block in zip(far, blocks)]]
    nears = [send(block, k, parties) for k, block in enumerate(nears)]
    for blocks in late:
        got.append([send(block, k, parties) for k, block in zip(far, split(blocks))])
    result = None
    for (first, count), blocks in zip(chunks, got):
        result = inverse(me, inverse_table, nears, blocks, first, count, result)
    return result


def solution(mesh):
    in_specs = (
        P(None, ("groups", "wide"), "narrow"),
        P(("groups", "wide"), None),
        P(("groups", "wide"), None),
        P(("groups", "wide"), "narrow", None, None, None),
    )
    out_specs = P(None, ("groups", "wide"), "narrow")
    return jax.shard_map(shards, mesh=mesh, in_specs=in_specs, out_specs=out_specs, check_vma=False)
```

```python
import functools
import math

import jax
import jax.numpy as jnp
import numpy as np
from jax import lax
from jax.experimental import pallas as pl
from jax.experimental.pallas import tpu as pltpu
from jax.sharding import PartitionSpec as P

BF16 = jnp.bfloat16
F32 = jnp.float32
SUB = 16
LANES = 128
MAXROW = 8
CUTS = (1, 1)


def even_terms(samples):
    return -(-(samples // 2 + 1) * SUB // LANES) * LANES // SUB


def transform_tables(samples, frequencies):
    turns = (1 + np.arange(frequencies))[:, None] * np.arange(samples)[None, :] % samples
    phases = turns * (2.0 * math.pi / samples)
    both = np.stack([np.cos(phases), -np.sin(phases)], axis=1) * samples**-0.5
    small = both.astype(jnp.bfloat16)
    twice = (2.0 * both).astype(jnp.bfloat16)
    half = samples // 2
    even = np.zeros((frequencies, SUB, even_terms(samples), SUB), jnp.bfloat16)
    odd = np.zeros((frequencies, SUB, half, SUB), jnp.bfloat16)
    inverse = np.zeros((samples, SUB, frequencies, 2, SUB), jnp.bfloat16)
    for r in range(SUB):
        even[:, r, : half + 1, r] = small[:, 0, : half + 1]
        odd[:, r, 1:, r] = small[:, 1, 1:half]
        inverse[:, r, :, :, r] = twice.transpose(2, 0, 1)

    def cut(table, high):
        table = table.reshape(high, -1, LANES)
        return np.ascontiguousarray(table.transpose(1, 0, 2))

    forward = np.concatenate([cut(even, frequencies * SUB), cut(odd, frequencies * SUB)])
    return forward, cut(inverse, samples * SUB)


def params(limit):
    return pltpu.CompilerParams(vmem_limit_bytes=min(limit, 56 * 2**20))


def place_of(me, k, rows, first, count):
    return pl.ds(pl.multiple_of((me ^ k) * rows + first, SUB), count)


def forward_kernel(first, step, me_ref, table_hbm, traces_hbm, *refs):
    early_refs = refs[:1] if first else ()
    near_ref, *far_refs = refs[len(early_refs) : -4]
    near = near_ref.shape[0]
    table_ref, traces_ref, table_sem, sems = refs[-4:]
    steps, samples, _, width = traces_ref.shape
    tiles, high, _ = table_ref.shape
    part = min(128, high)
    me = me_ref[0]

    def fetch(i):
        return pltpu.make_async_copy(
            traces_hbm.at[:, pl.ds(first + i * step, step), :], traces_ref.at[i], sems.at[i]
        )

    table_copy = pltpu.make_async_copy(table_hbm, table_ref, table_sem)
    table_copy.start()
    for i in range(steps):
        fetch(i).start()
    for ref in early_refs:
        near_ref[:, :, :first, :] = ref[...]
    table_copy.wait()

    @pl.loop(0, steps)
    def _(i):
        fetch(i).wait()

        def sample(t, b):
            return traces_ref[i, t, b : b + SUB, :]

        def even(t, b):
            if t in (0, half):
                return sample(t, b)
            return sample(t, b) + sample(samples - t, b) if t < half else empty

        def odd(t, b):
            return sample(t, b) - sample(samples - t, b) if t else empty

        half = samples // 2
        empty = jnp.zeros((SUB, width), BF16)
        cosines = even_terms(samples) * SUB // LANES
        for c, (fold, terms, pieces) in enumerate(
            (
                (even, even_terms(samples), range(cosines)),
                (odd, half, range(cosines, tiles)),
            )
        ):
            columns = jnp.concatenate(
                [
                    jnp.concatenate([fold(t, b) for t in range(terms)], axis=0)
                    for b in range(0, step, SUB)
                ],
                axis=1,
            )
            for low in range(0, high, part):
                group = range(low // SUB, (low + part) // SUB)
                table = jnp.concatenate(
                    [
                        jnp.concatenate(
                            [table_ref[k, place_of(me, s, SUB, 0, SUB), :] for s in group], axis=0
                        )
                        for k in pieces
                    ],
                    axis=1,
                )
                found = jnp.dot(table, columns, preferred_element_type=F32).astype(BF16)
                for s in group:
                    ref, begin = (near_ref.at[s], first) if s < near else (far_refs[s - near], 0)
                    row = s * SUB - low
                    for b in range(step // SUB):
                        spot = pl.ds(pl.multiple_of(begin + i * step + b * SUB, SUB), SUB)
                        ref[c, spot, :] = found[row : row + SUB, width * b : width * (b + 1)]


def forward(me, table, traces, near, first, count, early):
    samples, _, width = traces.shape
    parties = table.shape[1] // SUB
    step = min(2 * SUB, count)
    extra = [early] if first else []
    shapes = [(near, 2, first + count, width)] + [(2, count, width)] * (parties - near)
    return pl.pallas_call(
        functools.partial(forward_kernel, first, step),
        in_specs=[pl.BlockSpec(memory_space=pltpu.SMEM)]
        + [pl.BlockSpec(memory_space=pltpu.HBM)] * 2
        + [pl.BlockSpec(memory_space=pltpu.VMEM)] * len(extra),
        out_specs=[pl.BlockSpec(memory_space=pltpu.VMEM)] * len(shapes),
        scratch_shapes=[
            pltpu.VMEM(table.shape, BF16),
            pltpu.VMEM((count // step, samples, step, width), BF16),
            pltpu.SemaphoreType.DMA,
            pltpu.SemaphoreType.DMA((count // step,)),
        ],
        out_shape=[jax.ShapeDtypeStruct(shape, BF16) for shape in shapes],
        compiler_params=params(52 * 2**20),
        cost_estimate=pl.CostEstimate(
            flops=table.shape[1] * 4 * samples * width * count,
            bytes_accessed=2 * samples * count * width,
            transcendentals=0,
        ),
        name="forward",
    )(me, table, traces, *extra)


def tiles_kernel(near, chunks, block, count_ref, column_ref, place_ref, own_hbm, other_hbm, *refs):
    rows, width = refs[0].shape[1:]
    far = (len(refs) - 6 - 2 * near) // (2 * len(chunks))
    ins = near + far * len(chunks)
    near_in, far_in = refs[:near], refs[near:ins]
    near_out, far_out = refs[ins : ins + near], refs[ins + near : -6]
    tile_ref, top_ref, low_ref, sum_ref, row_ref, sems = refs[-6:]
    _, halves, _, size, _ = tile_ref.shape
    steps = halves // block
    me, side = place_ref[0], place_ref[1]
    tile_rows = count_ref.shape[1]

    def fetch(which, q):
        source = (own_hbm, other_hbm)[which]
        part = pl.ds(q * block, block)
        return pltpu.make_async_copy(source.at[part], tile_ref.at[which, part], sems.at[which, q])

    for q in range(steps):
        for which in range(2):
            fetch(which, q).start()

    for slot in range(2 * halves):
        row_ref[slot] = tile_rows
    begin = jnp.int32(0)
    for row in range(tile_rows + 1):
        for k in range(MAXROW):
            row_ref[begin + k] = row
        begin += count_ref[0, row] if row < tile_rows else 0

    def take(k, first, count, ref):
        place = place_of(me, k, rows, first, count)
        top_ref[place, :width] = ref[0]
        top_ref[place, width:] = ref[1]
        low_ref[place, :width] = -ref[1]
        low_ref[place, width:] = ref[0]

    def give(k, first, count, ref):
        place = place_of(me, k, rows, first, count)
        ref[0] = sum_ref[place, :width].astype(BF16)
        ref[1] = sum_ref[place, width:].astype(BF16)

    for k in range(near):
        take(k, 0, rows, near_in[k])
    for q, (first, count) in enumerate(chunks):
        for j in range(far):
            take(near + j, first, count, far_in[q * far + j])
    sum_ref[...] = jnp.zeros_like(sum_ref)

    @pl.loop(0, steps)
    def _(q):
        for which in range(2):
            fetch(which, q).wait()
        for k in range(block):
            for which in range(2):
                slot = q * block + k
                own = (side ^ which) * halves + slot
                column = jnp.clip(column_ref[0, own], 0, tile_rows - 1)
                place = pl.ds(pl.multiple_of(column * size, size), size)
                pair = jnp.concatenate(
                    [tile_ref[which, slot, 0], tile_ref[which, slot, 1]], axis=1
                )
                weights = jnp.concatenate([top_ref[place, :], low_ref[place, :]], axis=0)
                spot = pl.ds(pl.multiple_of(row_ref[own] * size, size), size)
                sum_ref[spot, :] += jnp.dot(pair, weights, preferred_element_type=F32)

    for k in range(near):
        give(k, 0, rows, near_out[k])
    for q, (first, count) in enumerate(chunks):
        for j in range(far):
            give(near + j, first, count, far_out[q * far + j])


def apply_tiles(counts, columns, place, own, other, chunks, nears, fars):
    halves, _, size, _ = own.shape
    _, rows, width = nears[0].shape
    far = len(fars) // len(chunks)
    total = (len(nears) + far) * rows
    block = math.gcd(20, halves)
    shapes = [nears[0].shape] * len(nears)
    shapes += [(2, part, width) for _, part in chunks for _ in range(far)]
    return pl.pallas_call(
        functools.partial(tiles_kernel, len(nears), chunks, block),
        in_specs=[pl.BlockSpec(memory_space=pltpu.SMEM)] * 3
        + [pl.BlockSpec(memory_space=pltpu.HBM)] * 2
        + [pl.BlockSpec(memory_space=pltpu.VMEM)] * (len(nears) + len(fars)),
        out_specs=[pl.BlockSpec(memory_space=pltpu.VMEM)] * len(shapes),
        scratch_shapes=[
            pltpu.VMEM((2,) + own.shape, BF16),
            pltpu.VMEM((total, 2 * width), BF16),
            pltpu.VMEM((total, 2 * width), BF16),
            pltpu.VMEM((total + size, 2 * width), F32),
            pltpu.SMEM((2 * halves + MAXROW,), jnp.int32),
            pltpu.SemaphoreType.DMA((2, halves // block)),
        ],
        out_shape=[jax.ShapeDtypeStruct(shape, BF16) for shape in shapes],
        compiler_params=params(28 * 2**20),
        cost_estimate=pl.CostEstimate(
            flops=2 * 2 * halves * size * 4 * size * width,
            bytes_accessed=4 * own.size,
            transcendentals=0,
        ),
        name="tiles",
    )(counts, columns, place, own, other, *nears, *fars)


def split_kernel(in_ref, *out_refs):
    for j, ref in enumerate(out_refs):
        ref[...] = in_ref[j]


def split(late):
    return pl.pallas_call(
        split_kernel,
        in_specs=[pl.BlockSpec(memory_space=pltpu.VMEM)],
        out_specs=[pl.BlockSpec(memory_space=pltpu.VMEM)] * late.shape[0],
        out_shape=[jax.ShapeDtypeStruct(late.shape[1:], BF16)] * late.shape[0],
        compiler_params=params(50 * 2**20),
        cost_estimate=pl.CostEstimate(flops=0, bytes_accessed=1 << 24, transcendentals=0),
        name="split",
    )(late)


def inverse_kernel(first, step, parties, near, me_ref, table_ref, *refs):
    in_refs = refs[:parties]
    out_hbm, column_ref, held_ref, sems = refs[-4:]
    steps, samples, _, width = held_ref.shape
    part = min(4096, samples * SUB)
    me = me_ref[0]

    def send(i):
        return pltpu.make_async_copy(
            held_ref.at[i], out_hbm.at[:, pl.ds(first + i * step, step), :], sems.at[i]
        )

    @pl.loop(0, steps)
    def _(i):
        for s in range(parties):
            for c in range(2):
                for b in range(step // SUB):
                    ref, begin = in_refs[s], first if s < near else 0
                    spot = pl.ds(pl.multiple_of(begin + i * step + b * SUB, SUB), SUB)
                    column_ref[
                        place_of(me, s, 2 * SUB, c * SUB, SUB), width * b : width * (b + 1)
                    ] = ref[c, spot, :]
        for low in range(0, samples * SUB, part):
            table = jnp.concatenate(
                [table_ref[k, low : low + part, :] for k in range(table_ref.shape[0])], axis=1
            )
            found = jnp.dot(table, column_ref[...], preferred_element_type=F32).astype(BF16)
            for b in range(step // SUB):
                held_ref[i, low // SUB : (low + part) // SUB, SUB * b : SUB * (b + 1), :] = found[
                    :, width * b : width * (b + 1)
                ].reshape(part // SUB, SUB, width)
        send(i).start()

    for i in range(steps):
        send(i).wait()


def inverse(me, table, nears, fars, first, count, filled):
    _, rows, width = nears[0].shape
    parties = len(nears) + len(fars)
    samples = table.shape[1] // SUB
    step = min(2 * SUB, count)
    extra = [] if filled is None else [filled]
    return pl.pallas_call(
        functools.partial(inverse_kernel, first, step, parties, len(nears)),
        in_specs=[pl.BlockSpec(memory_space=pltpu.SMEM)]
        + [pl.BlockSpec(memory_space=pltpu.VMEM)] * (1 + parties)
        + [pl.BlockSpec(memory_space=pl.ANY)] * len(extra),
        out_specs=pl.BlockSpec(memory_space=pl.ANY),
        scratch_shapes=[
            pltpu.VMEM((parties * 2 * SUB, step // SUB * width), BF16),
            pltpu.VMEM((count // step, samples, step, width), BF16),
            pltpu.SemaphoreType.DMA((count // step,)),
        ],
        out_shape=jax.ShapeDtypeStruct((samples, rows, width), BF16),
        input_output_aliases={2 + parties: 0} if extra else {},
        compiler_params=params(
            2 * samples * (SUB * LANES * table.shape[0] * 5 // 4 + count * width) + 14 * 2**20
        ),
        cost_estimate=pl.CostEstimate(
            flops=parties * 4 * SUB * samples * width * count,
            bytes_accessed=2 * samples * count * width,
            transcendentals=0,
        ),
        name="inverse",
    )(me, table, *nears, *fars, *extra)


def send(block, k, parties):
    return lax.ppermute(block, "wide", [(i, i ^ k) for i in range(parties)]) if k else block


def cuts(rows, sizes):
    if rows % (sum(sizes) * 2 * SUB):
        return ((0, rows),)
    unit = rows // sum(sizes)
    return tuple((unit * sum(sizes[:i]), unit * n) for i, n in enumerate(sizes))


def shards(traces, row_counts, tile_cols, tiles):
    samples, rows, _ = traces.shape
    parties = lax.axis_size("wide")
    forward_table, inverse_table = transform_tables(samples, parties)
    me = jnp.stack([lax.axis_index("wide"), lax.axis_index("narrow")]).astype(jnp.int32)
    chunks = cuts(rows, CUTS)
    near = parties // 2
    far = range(near, parties)

    early = None
    got = []
    for first, count in chunks:
        early, *blocks = forward(me, forward_table, traces, near, first, count, early)
        if not first:
            own_tiles, early = lax.optimization_barrier((tiles[0], early))
        got += [send(block, k, parties) for k, block in zip(far, blocks)]
    other = lax.ppermute(own_tiles, "narrow", [(0, 1), (1, 0)])
    other, early = lax.optimization_barrier((other, early))
    nears = [send(block, k, parties) for k, block in enumerate(split(early))]

    sums = apply_tiles(row_counts, tile_cols, me, own_tiles, other, chunks, nears, got)
    nears, blocks = sums[:near], sums[near:]
    nears = [send(block, k, parties) for k, block in enumerate(nears)]
    got = [
        [send(block, k, parties) for k, block in zip(far, blocks[q * len(far) :])]
        for q in range(len(chunks))
    ]
    result = None
    for (first, count), blocks in zip(chunks, got):
        result = inverse(me, inverse_table, nears, blocks, first, count, result)
    return result


def solution(mesh):
    in_specs = (
        P(None, ("groups", "wide"), "narrow"),
        P(("groups", "wide"), None),
        P(("groups", "wide"), None),
        P(("groups", "wide"), "narrow", None, None, None),
    )
    out_specs = P(None, ("groups", "wide"), "narrow")
    return jax.shard_map(shards, mesh=mesh, in_specs=in_specs, out_specs=out_specs, check_vma=False)
```

```python
import functools
import math

import jax
import jax.numpy as jnp
import numpy as np
from jax import lax
from jax.experimental import pallas as pl
from jax.experimental.pallas import tpu as pltpu
from jax.sharding import PartitionSpec as P

BF16 = jnp.bfloat16
F32 = jnp.float32
SUB = 16
LANES = 128
MAXROW = 8
CUTS = (1, 1)


def even_terms(samples):
    return -(-(samples // 2 + 1) * SUB // LANES) * LANES // SUB


def transform_tables(samples, frequencies):
    turns = (1 + np.arange(frequencies))[:, None] * np.arange(samples)[None, :] % samples
    phases = turns * (2.0 * math.pi / samples)
    both = np.stack([np.cos(phases), -np.sin(phases)], axis=1) * samples**-0.5
    small = both.astype(jnp.bfloat16)
    twice = (2.0 * both).astype(jnp.bfloat16)
    half = samples // 2
    even = np.zeros((frequencies, SUB, even_terms(samples), SUB), jnp.bfloat16)
    odd = np.zeros((frequencies, SUB, half, SUB), jnp.bfloat16)
    inverse = np.zeros((samples, SUB, frequencies, 2, SUB), jnp.bfloat16)
    for r in range(SUB):
        even[:, r, : half + 1, r] = small[:, 0, : half + 1]
        odd[:, r, 1:, r] = small[:, 1, 1:half]
        inverse[:, r, :, :, r] = twice.transpose(2, 0, 1)

    def cut(table, high):
        table = table.reshape(high, -1, LANES)
        return np.ascontiguousarray(table.transpose(1, 0, 2))

    forward = np.concatenate([cut(even, frequencies * SUB), cut(odd, frequencies * SUB)])
    return forward, cut(inverse, samples * SUB)


def params(limit):
    return pltpu.CompilerParams(vmem_limit_bytes=min(limit, 56 * 2**20))


def place_of(me, k, rows, first, count):
    return pl.ds(pl.multiple_of((me ^ k) * rows + first, SUB), count)


def forward_kernel(first, step, me_ref, table_hbm, traces_hbm, *refs):
    early_refs = refs[:1] if first else ()
    near_ref, *far_refs = refs[len(early_refs) : -4]
    near = near_ref.shape[0]
    table_ref, traces_ref, table_sem, sems = refs[-4:]
    steps, samples, _, width = traces_ref.shape
    tiles, high, _ = table_ref.shape
    part = min(128, high)
    me = me_ref[0]

    def fetch(i):
        return pltpu.make_async_copy(
            traces_hbm.at[:, pl.ds(first + i * step, step), :], traces_ref.at[i], sems.at[i]
        )

    table_copy = pltpu.make_async_copy(table_hbm, table_ref, table_sem)
    table_copy.start()
    for i in range(steps):
        fetch(i).start()
    for ref in early_refs:
        near_ref[:, :, :first, :] = ref[...]
    table_copy.wait()

    @pl.loop(0, steps)
    def _(i):
        fetch(i).wait()

        def sample(t, b):
            return traces_ref[i, t, b : b + SUB, :]

        def even(t, b):
            if t in (0, half):
                return sample(t, b)
            return sample(t, b) + sample(samples - t, b) if t < half else empty

        def odd(t, b):
            return sample(t, b) - sample(samples - t, b) if t else empty

        half = samples // 2
        empty = jnp.zeros((SUB, width), BF16)
        cosines = even_terms(samples) * SUB // LANES
        for c, (fold, terms, pieces) in enumerate(
            (
                (even, even_terms(samples), range(cosines)),
                (odd, half, range(cosines, tiles)),
            )
        ):
            columns = jnp.concatenate(
                [
                    jnp.concatenate([fold(t, b) for t in range(terms)], axis=0)
                    for b in range(0, step, SUB)
                ],
                axis=1,
            )
            for low in range(0, high, part):
                group = range(low // SUB, (low + part) // SUB)
                table = jnp.concatenate(
                    [
                        jnp.concatenate(
                            [table_ref[k, place_of(me, s, SUB, 0, SUB), :] for s in group], axis=0
                        )
                        for k in pieces
                    ],
                    axis=1,
                )
                found = jnp.dot(table, columns, preferred_element_type=F32).astype(BF16)
                for s in group:
                    ref, begin = (near_ref.at[s], first) if s < near else (far_refs[s - near], 0)
                    row = s * SUB - low
                    for b in range(step // SUB):
                        spot = pl.ds(pl.multiple_of(begin + i * step + b * SUB, SUB), SUB)
                        ref[c, spot, :] = found[row : row + SUB, width * b : width * (b + 1)]


def forward(me, table, traces, near, first, count, early):
    samples, _, width = traces.shape
    parties = table.shape[1] // SUB
    step = min(2 * SUB, count)
    extra = [early] if first else []
    shapes = [(near, 2, first + count, width)] + [(2, count, width)] * (parties - near)
    return pl.pallas_call(
        functools.partial(forward_kernel, first, step),
        in_specs=[pl.BlockSpec(memory_space=pltpu.SMEM)]
        + [pl.BlockSpec(memory_space=pl.ANY)] * 2
        + [pl.BlockSpec(memory_space=pltpu.VMEM)] * len(extra),
        out_specs=[pl.BlockSpec(memory_space=pltpu.VMEM)] * len(shapes),
        scratch_shapes=[
            pltpu.VMEM(table.shape, BF16),
            pltpu.VMEM((count // step, samples, step, width), BF16),
            pltpu.SemaphoreType.DMA,
            pltpu.SemaphoreType.DMA((count // step,)),
        ],
        out_shape=[jax.ShapeDtypeStruct(shape, BF16) for shape in shapes],
        compiler_params=params(52 * 2**20),
        cost_estimate=pl.CostEstimate(
            flops=table.shape[1] * 4 * samples * width * count,
            bytes_accessed=2 * samples * count * width,
            transcendentals=0,
        ),
        name="forward",
    )(me, table, traces, *extra)


def tiles_kernel(near, chunks, block, count_ref, column_ref, place_ref, own_hbm, other_hbm, *refs):
    rows, width = refs[0].shape[1:]
    far = refs[-7].shape[0] if len(chunks) > 1 else (len(refs) - 6) // 2 - near
    ins = near + far * len(chunks)
    near_in, far_in = refs[:near], refs[near:ins]
    near_out, far_out = refs[ins : ins + near], refs[ins + near : -6]
    tile_ref, top_ref, low_ref, sum_ref, row_ref, sems = refs[-6:]
    _, halves, _, size, _ = tile_ref.shape
    steps = halves // block
    me, side = place_ref[0], place_ref[1]
    tile_rows = count_ref.shape[1]

    def fetch(which, q):
        source = (own_hbm, other_hbm)[which]
        part = pl.ds(q * block, block)
        return pltpu.make_async_copy(source.at[part], tile_ref.at[which, part], sems.at[which, q])

    for q in range(steps):
        for which in range(2):
            fetch(which, q).start()

    for slot in range(2 * halves):
        row_ref[slot] = tile_rows
    begin = jnp.int32(0)
    for row in range(tile_rows + 1):
        for k in range(MAXROW):
            row_ref[begin + k] = row
        begin += count_ref[0, row] if row < tile_rows else 0

    def take(k, first, count, ref):
        place = place_of(me, k, rows, first, count)
        top_ref[place, :width] = ref[0]
        top_ref[place, width:] = ref[1]
        low_ref[place, :width] = -ref[1]
        low_ref[place, width:] = ref[0]

    def give(k, first, count, ref):
        place = place_of(me, k, rows, first, count)
        ref[0] = sum_ref[place, :width].astype(BF16)
        ref[1] = sum_ref[place, width:].astype(BF16)

    for k in range(near):
        take(k, 0, rows, near_in[k])
    for q, (first, count) in enumerate(chunks):
        for j in range(far):
            take(near + j, first, count, far_in[q * far + j])
    sum_ref[...] = jnp.zeros_like(sum_ref)

    @pl.loop(0, steps)
    def _(q):
        for which in range(2):
            fetch(which, q).wait()
        for k in range(block):
            for which in range(2):
                slot = q * block + k
                own = (side ^ which) * halves + slot
                column = jnp.clip(column_ref[0, own], 0, tile_rows - 1)
                place = pl.ds(pl.multiple_of(column * size, size), size)
                pair = jnp.concatenate(
                    [tile_ref[which, slot, 0], tile_ref[which, slot, 1]], axis=1
                )
                weights = jnp.concatenate([top_ref[place, :], low_ref[place, :]], axis=0)
                spot = pl.ds(pl.multiple_of(row_ref[own] * size, size), size)
                sum_ref[spot, :] += jnp.dot(pair, weights, preferred_element_type=F32)

    for k in range(near):
        give(k, 0, rows, near_out[k])
    for j in range(far):
        give(near + j, *chunks[0], far_out[j])
    for ref in far_out[far:]:
        for j in range(far):
            give(near + j, *chunks[1], ref.at[j])


def apply_tiles(counts, columns, place, own, other, chunks, nears, fars):
    halves, _, size, _ = own.shape
    _, rows, width = nears[0].shape
    far = len(fars) // len(chunks)
    total = (len(nears) + far) * rows
    block = math.gcd(40, halves)
    shapes = [nears[0].shape] * len(nears) + [(2, chunks[0][1], width)] * far
    shapes += [(far, 2, part, width) for _, part in chunks[1:]]
    return pl.pallas_call(
        functools.partial(tiles_kernel, len(nears), chunks, block),
        in_specs=[pl.BlockSpec(memory_space=pltpu.SMEM)] * 3
        + [pl.BlockSpec(memory_space=pl.ANY)] * 2
        + [pl.BlockSpec(memory_space=pltpu.VMEM)] * (len(nears) + len(fars)),
        out_specs=[pl.BlockSpec(memory_space=pltpu.VMEM)] * len(shapes),
        scratch_shapes=[
            pltpu.VMEM((2,) + own.shape, BF16),
            pltpu.VMEM((total, 2 * width), BF16),
            pltpu.VMEM((total, 2 * width), BF16),
            pltpu.VMEM((total + size, 2 * width), F32),
            pltpu.SMEM((2 * halves + MAXROW,), jnp.int32),
            pltpu.SemaphoreType.DMA((2, halves // block)),
        ],
        out_shape=[jax.ShapeDtypeStruct(shape, BF16) for shape in shapes],
        compiler_params=params(28 * 2**20),
        cost_estimate=pl.CostEstimate(
            flops=2 * 2 * halves * size * 4 * size * width,
            bytes_accessed=4 * own.size,
            transcendentals=0,
        ),
        name="tiles",
    )(counts, columns, place, own, other, *nears, *fars)


def split_kernel(in_ref, *out_refs):
    for j, ref in enumerate(out_refs):
        ref[...] = in_ref[j]


def split(late):
    return pl.pallas_call(
        split_kernel,
        in_specs=[pl.BlockSpec(memory_space=pltpu.VMEM)],
        out_specs=[pl.BlockSpec(memory_space=pltpu.VMEM)] * late.shape[0],
        out_shape=[jax.ShapeDtypeStruct(late.shape[1:], BF16)] * late.shape[0],
        compiler_params=params(50 * 2**20),
        cost_estimate=pl.CostEstimate(flops=0, bytes_accessed=1 << 24, transcendentals=0),
        name="split",
    )(late)


def inverse_kernel(first, step, parties, near, me_ref, table_ref, *refs):
    in_refs = refs[:parties]
    out_hbm, column_ref, held_ref, sems = refs[-4:]
    steps, samples, _, width = held_ref.shape
    part = min(4096, samples * SUB)
    me = me_ref[0]

    def send(i):
        return pltpu.make_async_copy(
            held_ref.at[i], out_hbm.at[:, pl.ds(first + i * step, step), :], sems.at[i]
        )

    @pl.loop(0, steps)
    def _(i):
        for s in range(parties):
            for c in range(2):
                for b in range(step // SUB):
                    ref, begin = in_refs[s], first if s < near else 0
                    spot = pl.ds(pl.multiple_of(begin + i * step + b * SUB, SUB), SUB)
                    column_ref[
                        place_of(me, s, 2 * SUB, c * SUB, SUB), width * b : width * (b + 1)
                    ] = ref[c, spot, :]
        for low in range(0, samples * SUB, part):
            table = jnp.concatenate(
                [table_ref[k, low : low + part, :] for k in range(table_ref.shape[0])], axis=1
            )
            found = jnp.dot(table, column_ref[...], preferred_element_type=F32).astype(BF16)
            for b in range(step // SUB):
                held_ref[i, low // SUB : (low + part) // SUB, SUB * b : SUB * (b + 1), :] = found[
                    :, width * b : width * (b + 1)
                ].reshape(part // SUB, SUB, width)
        send(i).start()

    for i in range(steps):
        send(i).wait()


def inverse(me, table, nears, fars, first, count, filled):
    _, rows, width = nears[0].shape
    parties = len(nears) + len(fars)
    samples = table.shape[1] // SUB
    step = min(2 * SUB, count)
    extra = [] if filled is None else [filled]
    return pl.pallas_call(
        functools.partial(inverse_kernel, first, step, parties, len(nears)),
        in_specs=[pl.BlockSpec(memory_space=pltpu.SMEM)]
        + [pl.BlockSpec(memory_space=pltpu.VMEM)] * (1 + parties)
        + [pl.BlockSpec(memory_space=pl.ANY)] * len(extra),
        out_specs=pl.BlockSpec(memory_space=pl.ANY),
        scratch_shapes=[
            pltpu.VMEM((parties * 2 * SUB, step // SUB * width), BF16),
            pltpu.VMEM((count // step, samples, step, width), BF16),
            pltpu.SemaphoreType.DMA((count // step,)),
        ],
        out_shape=jax.ShapeDtypeStruct((samples, rows, width), BF16),
        input_output_aliases={2 + parties: 0} if extra else {},
        compiler_params=params(
            2 * samples * (SUB * LANES * table.shape[0] * 5 // 4 + count * width) + 14 * 2**20
        ),
        cost_estimate=pl.CostEstimate(
            flops=parties * 4 * SUB * samples * width * count,
            bytes_accessed=2 * samples * count * width,
            transcendentals=0,
        ),
        name="inverse",
    )(me, table, *nears, *fars, *extra)


def send(block, k, parties):
    return lax.ppermute(block, "wide", [(i, i ^ k) for i in range(parties)]) if k else block


def cuts(rows, sizes):
    if rows % (sum(sizes) * 2 * SUB):
        return ((0, rows),)
    unit = rows // sum(sizes)
    return tuple((unit * sum(sizes[:i]), unit * n) for i, n in enumerate(sizes))


def shards(traces, row_counts, tile_cols, tiles):
    samples, rows, _ = traces.shape
    parties = lax.axis_size("wide")
    forward_table, inverse_table = transform_tables(samples, parties)
    me = jnp.stack([lax.axis_index("wide"), lax.axis_index("narrow")]).astype(jnp.int32)
    chunks = cuts(rows, CUTS)
    near = parties // 2
    far = range(near, parties)

    early = None
    got = []
    for first, count in chunks:
        early, *blocks = forward(me, forward_table, traces, near, first, count, early)
        got += [send(block, k, parties) for k, block in zip(far, blocks)]
    other = lax.ppermute(tiles[0], "narrow", [(0, 1), (1, 0)])
    other, early = lax.optimization_barrier((other, early))
    nears = [send(block, k, parties) for k, block in enumerate(split(early))]

    sums = apply_tiles(row_counts, tile_cols, me, tiles[0], other, chunks, nears, got)
    nears, blocks, late = sums[:near], sums[near:parties], sums[parties:]
    got = [[send(block, k, parties) for k, block in zip(far, blocks)]]
    nears = [send(block, k, parties) for k, block in enumerate(nears)]
    for blocks in late:
        got.append([send(block, k, parties) for k, block in zip(far, split(blocks))])
    result = None
    for (first, count), blocks in zip(chunks, got):
        result = inverse(me, inverse_table, nears, blocks, first, count, result)
    return result


def solution(mesh):
    in_specs = (
        P(None, ("groups", "wide"), "narrow"),
        P(("groups", "wide"), None),
        P(("groups", "wide"), None),
        P(("groups", "wide"), "narrow", None, None, None),
    )
    out_specs = P(None, ("groups", "wide"), "narrow")
    return jax.shard_map(shards, mesh=mesh, in_specs=in_specs, out_specs=out_specs, check_vma=False)
```
